512 devices in a mesh: tok: 16 (over x, z_hi), feat: 32 (over y, z_lo, core).
Axes of the slice: x: 4, y: 4, z: 16 (z_hi: 4, z_lo: 4; z = z_hi * 4 + z_lo), core: 2. Of those that a mesh axis runs over, the one named last changes fastest.
Arguments:
- layer_inputs: bfloat16 [2048, 4096], P('tok', 'feat'), may hold values from -6 to 6
- output_grads: bfloat16 [2048, 8192], P('tok', 'feat'), may hold values from -6 to 6
- input_factor: float32 [4096, 4096], P('tok', 'feat'), may hold values from -1 to 4, as said below
- output_factor: float32 [8192, 8192], P('tok', 'feat'), may hold values from -1 to 4, as said below
- input_inverse: bfloat16 [4096, 4096], P('tok', 'feat'), may hold values from -2 to 16, as said below
- output_inverse: bfloat16 [8192, 8192], P('tok', 'feat'), may hold values from -2 to 16, as said below
Outputs:
- input_running: float32 [4096, 4096], P('tok', 'feat')
- output_running: float32 [8192, 8192], P('tok', 'feat')
- natural_gradient: float32 [4096, 8192], P('tok', 'feat')
The draws below stay inside these ranges and needn't reach their ends.
Inputs may be any that keep to these rules, and one draw needn't show every extreme that they name: input_factor equals its transpose. output_factor equals its transpose. input_inverse equals its transpose. output_inverse equals its transpose.
All inputs are finite; a program needn't handle non-finite values.
Results may differ from the reference program's by a relative error of at most 0.0041.
Values may be sent and summed in bfloat16 or wider, within the bound.
No kernel may reach another device: no remote copies, remote signals or barrier semaphores. Data moves between devices by JAX's collectives and lax.ppermute only.
A program may use at most 64 MiB of HBM per device.

```python
import math
import jax
import jax.numpy as jnp
from jax import lax

D = 4096
F = 8192
TOKENS = 2048


def symmetric_field(key, extent, lowest, highest, spread):
    jitter_key, diagonal_key = jax.random.split(key)
    jitter_values = jnp.clip(jax.random.normal(jitter_key, (extent, extent), jnp.float32), -4.0, 4.0)
    jitter_values = 0.5 * (jitter_values + jitter_values.T) * (spread / math.sqrt(extent))
    diagonal_values = jnp.exp(jax.random.uniform(diagonal_key, (extent, 1), jnp.float32, math.log(lowest), math.log(highest)))
    row_index = lax.broadcasted_iota(jnp.int32, (extent, extent), 0)
    column_index = lax.broadcasted_iota(jnp.int32, (extent, extent), 1)
    return jnp.where(row_index == column_index, diagonal_values, jitter_values)


def draw_input_factor(key, part):
    key = jax.random.fold_in(key, 11)
    return symmetric_field(key, D, 0.5, 2.0, 0.5)


def draw_output_factor(key, part):
    key = jax.random.fold_in(key, 23)
    return symmetric_field(key, F, 0.5, 2.0, 0.5)


def draw_input_inverse(key, part):
    key = jax.random.fold_in(key, 37)
    return symmetric_field(key, D, 2.0, 8.0, 2.0).astype(jnp.bfloat16)


def draw_output_inverse(key, part):
    key = jax.random.fold_in(key, 41)
    return symmetric_field(key, F, 2.0, 8.0, 2.0).astype(jnp.bfloat16)


def block_scale(key, shape, cuts, smallest, high):
    def one(position, blocks):
        steps = jax.random.uniform(jax.random.fold_in(jax.random.fold_in(key, 6), position), (blocks,), jnp.float32, smallest / len(cuts), high / len(cuts))
        return jnp.repeat(jnp.exp(steps), shape[position] // blocks).reshape((-1,) + (1,) * (len(shape) - position - 1))

    loudness = one(*cuts[0])
    for cut in cuts[1:]:
        loudness = loudness * one(*cut)
    return loudness


def centred(key, shape, deviation, reach, shards=(), held_as=jnp.bfloat16):
    array = jax.random.normal(key, shape, jnp.float32) * deviation
    if len(shards) > 0:
        array = block_scale(key, shape, shards, -0.22, 0.18) * array
    return jnp.clip(array, min=-reach, max=reach).astype(held_as)


def setup_inputs(seed: int = 0) -> dict:
    key_of = jax.random.split(jax.random.key(seed), 7)
    return {
        "layer_inputs": centred(key_of[0], (TOKENS, D), 1.0, 6.0, ((0, 16), (1, 32))),
        "output_grads": centred(key_of[1], (TOKENS, F), 1.0, 6.0, ((0, 16), (1, 32))),
        "input_factor": draw_input_factor(jax.random.fold_in(key_of[6], 71), 0),
        "output_factor": draw_output_factor(jax.random.fold_in(key_of[6], 71), 0),
        "input_inverse": draw_input_inverse(jax.random.fold_in(key_of[6], 71), 0),
        "output_inverse": draw_output_inverse(jax.random.fold_in(key_of[6], 71), 0),
    }


stat_decay = 0.9


def reference(layer_inputs, output_grads, input_factor, output_factor, input_inverse, output_inverse):
    tokens = layer_inputs.shape[0]
    mixed_inputs = jnp.dot(layer_inputs, input_inverse, preferred_element_type=jnp.float32).astype(jnp.bfloat16)
    mixed_grads = jnp.dot(output_grads, output_inverse, preferred_element_type=jnp.float32).astype(jnp.bfloat16)
    input_batch = jnp.dot(layer_inputs.T, layer_inputs, preferred_element_type=jnp.float32) / tokens
    output_batch = jnp.dot(output_grads.T, output_grads, preferred_element_type=jnp.float32) / tokens
    input_running = stat_decay * input_factor + (1.0 - stat_decay) * input_batch
    output_running = stat_decay * output_factor + (1.0 - stat_decay) * output_batch
    natural_gradient = jnp.dot(mixed_inputs.T, mixed_grads, preferred_element_type=jnp.float32) / tokens
    return input_running, output_running, natural_gradient
```

```python
import jax
import jax.numpy as jnp
from jax import lax
from jax.sharding import Mesh, PartitionSpec as P

stat_decay = 0.9
by_rows = (((0,), (0,)), ((), ()))
by_cols = (((1,), (1,)), ((), ()))
TOK = ("x", "zh")
FEAT = ("y", "zl", "core")
SIDE = 4
CORES = 2


def swap_pairs():
    blocks = SIDE * SIDE
    pairs = []
    for a in range(blocks):
        for b in range(blocks):
            for c in range(CORES):
                pairs.append(((a * blocks + b) * CORES + c, (b * blocks + a) * CORES + c))
    return pairs


def gather(block, axis):
    return lax.all_gather(block, axis, axis=0, tiled=True)


def scatter_sum(partial, axis, wire):
    parts = partial.reshape(SIDE, partial.shape[0] // SIDE, partial.shape[1]).astype(wire)
    parts = lax.all_to_all(parts, axis, 0, 0)
    return jnp.sum(parts.astype(jnp.float32), axis=0)


def dot(left, right, dims):
    return lax.dot_general(left, right, dims, preferred_element_type=jnp.float32)


def per_device(
    layer_inputs, output_grads, input_factor, output_factor, input_inverse, output_inverse
):
    tokens = layer_inputs.shape[0] * SIDE * SIDE
    width = layer_inputs.shape[1]
    both = jnp.concatenate([layer_inputs, output_grads], axis=1)

    swapped = lax.ppermute(both, TOK + FEAT, swap_pairs())
    cols = gather(gather(both, "zh"), "x")
    rows = gather(gather(swapped, "zl"), "y")
    rows = lax.all_gather(rows, "core", axis=0, tiled=False)

    input_cols, output_cols = cols[:, :width], cols[:, width:]
    input_rows = jnp.concatenate([rows[0, :, :width], rows[1, :, :width]], axis=1)
    output_rows = jnp.concatenate([rows[0, :, width:], rows[1, :, width:]], axis=1)

    grads_part = dot(output_rows, output_inverse, (((1,), (0,)), ((), ())))
    grads_mixed = scatter_sum(scatter_sum(grads_part, "x", jnp.bfloat16), "zh", jnp.bfloat16)
    grads_mixed = gather(gather(grads_mixed.astype(jnp.bfloat16), "zh"), "x")

    halves = input_cols.reshape(CORES, tokens // CORES, width)
    halves = lax.all_to_all(halves, "core", 0, 0)
    inverse = lax.all_gather(input_inverse, "core", axis=0, tiled=False)
    input_part = dot(halves[0], inverse[0], by_cols) + dot(halves[1], inverse[1], by_cols)
    input_mixed = scatter_sum(scatter_sum(input_part, "y", jnp.float32), "zl", jnp.float32)
    input_mixed = gather(gather(input_mixed.astype(jnp.bfloat16), "zl"), "y")
    input_mixed = gather(input_mixed, "core")

    input_batch = dot(input_rows, input_cols, by_rows) / tokens
    output_batch = dot(output_rows, output_cols, by_rows) / tokens
    natural_gradient = dot(input_mixed, grads_mixed, by_rows) / tokens
    input_running = stat_decay * input_factor + (1.0 - stat_decay) * input_batch
    output_running = stat_decay * output_factor + (1.0 - stat_decay) * output_batch
    return (input_running, output_running, natural_gradient)


def solution(mesh):
    grid = Mesh(mesh.devices.reshape(SIDE, SIDE, SIDE, SIDE, CORES), TOK + FEAT)
    spec = P(TOK, FEAT)
    return jax.shard_map(
        per_device, mesh=grid, in_specs=(spec,) * 6, out_specs=(spec,) * 3, check_vma=False
    )
```

```python
import jax
import jax.numpy as jnp
from jax import lax
from jax.sharding import Mesh, PartitionSpec as P

stat_decay = 0.9
by_rows = (((0,), (0,)), ((), ()))
by_cols = (((1,), (1,)), ((), ()))
TOK = ("x", "zh")
FEAT = ("y", "zl", "core")
SIDE = 4
CORES = 2


def swap_pairs():
    blocks = SIDE * SIDE
    pairs = []
    for a in range(blocks):
        for b in range(blocks):
            for c in range(CORES):
                pairs.append(((a * blocks + b) * CORES + c, (b * blocks + a) * CORES + c))
    return pairs


def gather(block, axis):
    return lax.all_gather(block, axis, axis=0, tiled=True)


def scatter_sum(partial, axis, wire):
    parts = partial.reshape(SIDE, partial.shape[0] // SIDE, partial.shape[1]).astype(wire)
    parts = lax.all_to_all(parts, axis, 0, 0)
    return jnp.sum(parts.astype(jnp.float32), axis=0)


def dot(left, right, dims):
    return lax.dot_general(left, right, dims, preferred_element_type=jnp.float32)


def gather_direct(block, axis):
    count = lax.axis_size(axis)
    copies = jnp.broadcast_to(block[None], (count,) + block.shape)
    return lax.all_to_all(copies, axis, 0, 0).reshape(count * block.shape[0], block.shape[1])


def per_device(
    layer_inputs, output_grads, input_factor, output_factor, input_inverse, output_inverse
):
    tokens = layer_inputs.shape[0] * SIDE * SIDE
    width = layer_inputs.shape[1]
    grads_width = output_grads.shape[1]
    core = lax.axis_index("core")
    both = jnp.concatenate([layer_inputs, output_grads], axis=1)

    swapped = lax.ppermute(both, TOK + FEAT, swap_pairs())
    cols = gather(both, "zh")
    swapped, cols = lax.optimization_barrier((swapped, cols))
    cols = gather(cols, "x")
    rows = gather_direct(gather(swapped, "zl"), "y")
    other = lax.ppermute(rows, "core", [(0, 1), (1, 0)])

    input_cols, output_cols = cols[:, :width], cols[:, width:]
    own_inverse = lax.dynamic_slice_in_dim(output_inverse, core * grads_width, grads_width)
    other_inverse = lax.dynamic_slice_in_dim(
        output_inverse, (1 - core) * grads_width, grads_width
    )
    plain = (((1,), (0,)), ((), ()))
    grads_part = dot(rows[:, width:], own_inverse, plain) + dot(
        other[:, width:], other_inverse, plain
    )
    grads_mixed = scatter_sum(scatter_sum(grads_part, "x", jnp.bfloat16), "zh", jnp.bfloat16)
    grads_mixed = gather_direct(gather(grads_mixed.astype(jnp.bfloat16), "zh"), "x")

    halves = input_cols.reshape(CORES, tokens // CORES, width)
    halves = lax.all_to_all(halves, "core", 0, 0)
    inverse = lax.all_gather(input_inverse, "core", axis=0, tiled=False)
    input_part = dot(halves[0], inverse[0], by_cols) + dot(halves[1], inverse[1], by_cols)
    input_mixed = scatter_sum(scatter_sum(input_part, "y", jnp.float32), "zl", jnp.float32)
    input_mixed = gather(gather(input_mixed.astype(jnp.bfloat16), "zl"), "y")
    input_mixed = gather_direct(input_mixed, "core")

    def batch(own, far, columns):
        own = dot(own, columns, by_rows) / tokens
        far = dot(far, columns, by_rows) / tokens
        return jnp.where(
            core == 0, jnp.concatenate([own, far]), jnp.concatenate([far, own])
        )

    input_batch = batch(rows[:, :width], other[:, :width], input_cols)
    output_batch = batch(rows[:, width:], other[:, width:], output_cols)
    natural_gradient = dot(input_mixed, grads_mixed, by_rows) / tokens
    input_running = stat_decay * input_factor + (1.0 - stat_decay) * input_batch
    output_running = stat_decay * output_factor + (1.0 - stat_decay) * output_batch
    return (input_running, output_running, natural_gradient)


def solution(mesh):
    grid = Mesh(mesh.devices.reshape(SIDE, SIDE, SIDE, SIDE, CORES), TOK + FEAT)
    spec = P(TOK, FEAT)
    return jax.shard_map(
        per_device, mesh=grid, in_specs=(spec,) * 6, out_specs=(spec,) * 3, check_vma=False
    )
```

```python
import functools

import jax
import jax.numpy as jnp
from jax import lax
from jax.experimental import pallas as pl
from jax.experimental.pallas import tpu as pltpu
from jax.sharding import Mesh, PartitionSpec as P

stat_decay = 0.9
by_rows = (((0,), (0,)), ((), ()))
by_cols = (((1,), (1,)), ((), ()))
plain = (((1,), (0,)), ((), ()))
TOK = ("x", "zh")
FEAT = ("y", "zl", "core")
ALL = TOK + FEAT
SIDE = 4
CORES = 2
f32, bf16 = jnp.float32, jnp.bfloat16


def device(x, zh, y, zl, core):
    return (((x * SIDE + zh) * SIDE + y) * SIDE + zl) * CORES + core


def role_groups(first, second):
    groups = []
    for core, axis in ((0, first), (1, second)):
        others = [name for name in ALL[:4] if name != axis]
        for i in range(SIDE):
            for j in range(SIDE):
                for k in range(SIDE):
                    fixed = dict(zip(others, (i, j, k)))
                    groups.append(
                        [device(core=core, **fixed, **{axis: n}) for n in range(SIDE)]
                    )
    return groups


def swap_pairs():
    pairs = []
    for x in range(SIDE):
        for zh in range(SIDE):
            for y in range(SIDE):
                for zl in range(SIDE):
                    pairs.append((device(x, zh, y, zl, 0), device(x, zh, y, zl, 0)))
                    pairs.append((device(x, zh, y, zl, 1), device(y, zl, x, zh, 1)))
    return pairs


def ring_pairs(turn):
    pairs = []
    for group in role_groups("x", "y"):
        pairs += [(group[n], group[(n + turn) % SIDE]) for n in range(SIDE)]
    return pairs


def gather(block, groups):
    return lax.all_gather(block, ALL, axis_index_groups=groups, axis=0, tiled=False)


def exchange(parts, groups):
    return lax.all_to_all(parts, ALL, 0, 0, axis_index_groups=groups)


def gather_direct(block, groups):
    return exchange(jnp.broadcast_to(block[None], (SIDE,) + block.shape), groups)


def core_swap(block):
    return lax.ppermute(block, "core", [(0, 1), (1, 0)])


def dot(left, right, dims):
    return lax.dot_general(left, right, dims, preferred_element_type=f32)


def flat(block):
    return block.reshape(-1, block.shape[-1])


def local_call(body, out_shape, role, *operands, flops=0, steps=None, blocks=None):
    moved = sum(o.size * o.dtype.itemsize for o in operands)
    moved += sum(o.size * o.dtype.itemsize for o in jax.tree.leaves(out_shape))
    whole = pl.BlockSpec(memory_space=pltpu.VMEM)
    if steps is None:
        grid, in_blocks = (), [whole] * len(operands)
        out_blocks = jax.tree.map(lambda _: whole, out_shape)
    else:
        grid, in_blocks, out_blocks = (steps,), blocks[0], blocks[1]
    return pl.pallas_call(
        body,
        grid=grid,
        out_shape=out_shape,
        in_specs=[pl.BlockSpec(memory_space=pltpu.SMEM)] + in_blocks,
        out_specs=out_blocks,
        compiler_params=pltpu.CompilerParams(vmem_limit_bytes=24 * 1024 * 1024),
        cost_estimate=pl.CostEstimate(flops=flops, bytes_accessed=moved, transcendentals=0),
    )(role, *operands)


def block_at(shape, place):
    def index(step):
        return tuple(step if axis == place else 0 for axis in range(len(shape)))

    return pl.BlockSpec(shape, index)


def high_low(value):
    high = value.astype(bf16)
    return high, (value - high.astype(f32)).astype(bf16)


def partial_body(role, mine, in_inverse, out_inverse, out):
    deep = out_inverse.shape[1] // CORES

    @pl.when(role[0] == 0)
    def _():
        inverse = jnp.concatenate([in_inverse[0], in_inverse[1]], axis=1)
        high, low = high_low(dot(flat(mine[0, :, 0]), inverse, by_cols))
        out[0, 0] = high
        out[0, 1] = low

    @pl.when(role[0] == 1)
    def _():
        near, far = flat(mine[0, :, 0]), flat(mine[0, :, 1])
        for half in range(CORES):
            part = dot(near, out_inverse[half, :deep], plain)
            part = part + dot(far, out_inverse[half, deep:], plain)
            out[0, half] = part.astype(bf16)


def resum_body(role, parts, out):
    rows = out.shape[2]

    @pl.loop(0, SIDE)
    def _(i):
        at = pl.ds(pl.multiple_of(i * rows, rows), rows)
        totals = [
            sum(parts[k, half, at, :].astype(f32) for k in range(SIDE)) for half in range(CORES)
        ]

        @pl.when(role[0] == 0)
        def _():
            high, low = high_low(totals[0] + totals[1])
            out[i, 0] = high
            out[i, 1] = low

        @pl.when(role[0] == 1)
        def _():
            out[i, 0] = totals[0].astype(bf16)
            out[i, 1] = totals[1].astype(bf16)


def finish_body(role, parts, out):
    totals = [sum(parts[k, half].astype(f32) for k in range(SIDE)) for half in range(CORES)]

    @pl.when(role[0] == 0)
    def _():
        out[0] = (totals[0] + totals[1]).astype(bf16)
        out[1] = jnp.zeros_like(out[1])

    @pl.when(role[0] == 1)
    def _():
        out[0] = totals[0].astype(bf16)
        out[1] = totals[1].astype(bf16)


def natural_body(tokens, role, mixed, crossed, out):
    @pl.when(pl.program_id(0) == 0)
    def _():
        out[...] = jnp.zeros_like(out)

    @pl.when(role[0] == 0)
    def _():
        out[...] += dot(flat(mixed[0, :, 0]), flat(crossed[0]), by_rows) / tokens

    @pl.when(role[0] == 1)
    def _():
        out[...] += dot(flat(crossed[0]), flat(mixed[0, :, 1]), by_rows) / tokens


def running_body(role, mine, their, late, their_late, in_old, out_old, in_new, out_new):
    tokens = late.shape[0] * late.shape[1] * late.shape[2]
    width, wide = in_old.shape[1], out_old.shape[1]
    new_part = 1.0 - stat_decay

    def finish(in_rows, near_rows, far_rows, in_cols, out_cols):
        batch = sum(dot(in_rows(i), in_cols(i), by_rows) for i in range(SIDE)) / tokens
        in_new[...] = stat_decay * in_old[...] + new_part * batch
        for half, rows in ((0, near_rows), (1, far_rows)):
            at = pl.ds(half * wide, wide)
            batch = sum(dot(rows(i), out_cols(i), by_rows) for i in range(SIDE)) / tokens
            out_new[at, :] = stat_decay * out_old[at, :] + new_part * batch

    def part(ref, half, start=0, stop=None):
        return lambda i: flat(ref[i, :, half, :, start:stop])

    def turned(ref, spot):
        return lambda i: flat(ref[lax.rem(spot + (SIDE - i), SIDE)])

    @pl.when(role[0] == 0)
    def _():
        rows, cols = turned(their_late, role[2]), part(mine, 0, 0, width)
        finish(rows, part(their, 0), part(their, 1), cols, part(mine, 1))

    @pl.when(role[0] == 1)
    def _():
        rows, cols = turned(late, role[1]), part(their, 0, width)
        finish(rows, part(mine, 0), part(mine, 1), cols, turned(their_late, role[2]))


def per_device(
    layer_inputs, output_grads, input_factor, output_factor, input_inverse, output_inverse
):
    rows = layer_inputs.shape[0]
    wide = output_grads.shape[1]
    tokens = rows * SIDE * SIDE
    core = lax.axis_index("core")
    first = core == 0
    role = core.astype(jnp.int32).reshape(1)
    spot = (lax.axis_index("x"), lax.axis_index("y"))
    tied = lax.optimization_barrier

    out_z = role_groups("zh", "zl")
    out_xy = role_groups("x", "y")
    back_z = role_groups("zl", "zh")
    back_xy = role_groups("y", "x")

    grads_pair = lax.all_gather(output_grads, "core", axis=0, tiled=False)
    grads_moved = lax.ppermute(grads_pair, ALL, swap_pairs())
    grads_pair, layer_inputs = tied((grads_pair, layer_inputs))
    input_pair = lax.all_gather(layer_inputs, "core", axis=1, tiled=True)
    inputs_moved = lax.ppermute(input_pair, ALL, swap_pairs())

    block = jnp.where(first, jnp.stack([input_pair, grads_pair[0]]), grads_moved)
    block = gather(block, out_z)
    block, late, inputs_moved, input_inverse, output_inverse = tied(
        (block, grads_pair[1], inputs_moved, input_inverse, output_inverse)
    )
    mine = gather_direct(block, out_xy)
    in_inverse = lax.all_gather(input_inverse, "core", axis=0, tiled=False)
    out_inverse = lax.all_gather(output_inverse, "core", axis=0, tiled=False)

    part = local_call(
        partial_body,
        jax.ShapeDtypeStruct((SIDE, CORES, SIDE * rows, wide), bf16),
        role,
        mine,
        in_inverse,
        out_inverse,
        flops=2 * tokens * 4 * wide * wide,
        steps=SIDE,
        blocks=(
            [
                block_at((1, SIDE, CORES, rows, wide), 0),
                block_at(in_inverse.shape, None),
                block_at(out_inverse.shape, None),
            ],
            block_at((1, CORES, SIDE * rows, wide), 0),
        ),
    )
    part, late, inputs_moved = tied((part, late, inputs_moved))
    late = gather(jnp.where(first, late, inputs_moved), out_z)
    part = exchange(part, back_xy)
    part, late = tied((part, late))
    part = local_call(
        resum_body,
        jax.ShapeDtypeStruct((SIDE, CORES, rows, wide), bf16),
        role,
        part,
    )
    part, late = tied((part, late))
    part = exchange(part, back_z)
    left = lax.ppermute(late, ALL, ring_pairs(1))
    right = lax.ppermute(late, ALL, ring_pairs(-1))
    span = SIDE // CORES
    ahead = lax.ppermute(left[:span], ALL, ring_pairs(1))
    behind = lax.ppermute(right[span:], ALL, ring_pairs(-1))
    late = jnp.stack([late, left, jnp.concatenate([ahead, behind]), right])
    part, late = tied((part, late))
    mixed = local_call(
        finish_body, jax.ShapeDtypeStruct((CORES, rows, wide), bf16), role, part
    )
    mixed = gather(mixed, back_z)
    mixed, mine, late = tied((mixed, mine, late))
    mixed = gather_direct(mixed, back_xy)
    their, their_late = core_swap(mine), core_swap(late)
    input_running, output_running = local_call(
        running_body,
        (
            jax.ShapeDtypeStruct(input_factor.shape, f32),
            jax.ShapeDtypeStruct(output_factor.shape, f32),
        ),
        jnp.stack([core, jnp.where(first, spot[0], spot[1]), jnp.where(first, spot[1], spot[0])]),
        mine,
        their,
        late,
        their_late,
        input_factor,
        output_factor,
        flops=2 * tokens * (2 * wide * wide + wide * wide // 2),
    )
    mixed, input_running, output_running = tied((mixed, input_running, output_running))
    crossed = core_swap(mixed[:, :, 0])
    natural_gradient = local_call(
        functools.partial(natural_body, tokens),
        jax.ShapeDtypeStruct((wide, wide), f32),
        role,
        mixed,
        crossed,
        flops=2 * tokens * wide * wide,
        steps=SIDE,
        blocks=(
            [
                block_at((1, SIDE, CORES, rows, wide), 0),
                block_at((1, SIDE, rows, wide), 0),
            ],
            block_at((wide, wide), None),
        ),
    )
    return (input_running, output_running, natural_gradient)


def solution(mesh):
    grid = Mesh(mesh.devices.reshape(SIDE, SIDE, SIDE, SIDE, CORES), ALL)
    spec = P(TOK, FEAT)
    return jax.shard_map(
        per_device, mesh=grid, in_specs=(spec,) * 6, out_specs=(spec,) * 3, check_vma=False
    )
```

```python
import functools
import math

import jax
import jax.numpy as jnp
from jax import lax
from jax.experimental import pallas as pl
from jax.experimental.pallas import tpu as pltpu
from jax.sharding import Mesh, PartitionSpec as P

stat_decay = 0.9
by_rows = (((0,), (0,)), ((), ()))
by_cols = (((1,), (1,)), ((), ()))
plain = (((1,), (0,)), ((), ()))
TOK = ("x", "zh")
FEAT = ("y", "zl", "core")
ALL = TOK + FEAT
SIDE = 4
CORES = 2
f32, bf16 = jnp.float32, jnp.bfloat16


def device(x, zh, y, zl, core):
    return (((x * SIDE + zh) * SIDE + y) * SIDE + zl) * CORES + core


def role_groups(first, second):
    groups = []
    for core, axis in ((0, first), (1, second)):
        others = [name for name in ALL[:4] if name != axis]
        for i in range(SIDE):
            for j in range(SIDE):
                for k in range(SIDE):
                    fixed = dict(zip(others, (i, j, k)))
                    groups.append(
                        [device(core=core, **fixed, **{axis: n}) for n in range(SIDE)]
                    )
    return groups


def swap_pairs():
    pairs = []
    for x in range(SIDE):
        for zh in range(SIDE):
            for y in range(SIDE):
                for zl in range(SIDE):
                    pairs.append((device(x, zh, y, zl, 0), device(x, zh, y, zl, 0)))
                    pairs.append((device(x, zh, y, zl, 1), device(y, zl, x, zh, 1)))
    return pairs


def ring_pairs(turn):
    pairs = []
    for group in role_groups("x", "y"):
        pairs += [(group[n], group[(n + turn) % SIDE]) for n in range(SIDE)]
    return pairs


def gather(block, groups):
    return lax.all_gather(block, ALL, axis_index_groups=groups, axis=0, tiled=False)


def exchange(parts, groups):
    return lax.all_to_all(parts, ALL, 0, 0, axis_index_groups=groups)


def gather_direct(block, groups):
    return exchange(jnp.broadcast_to(block[None], (SIDE,) + block.shape), groups)


def core_swap(block):
    return lax.ppermute(block, "core", [(0, 1), (1, 0)])


def dot(left, right, dims):
    return lax.dot_general(left, right, dims, preferred_element_type=f32)


def flat(block):
    return block.reshape(-1, block.shape[-1])


def local_call(body, out_shape, role, *operands, flops=0, steps=None, blocks=None, out_blocks=None, scratch=()):
    moved = sum(o.size * o.dtype.itemsize for o in operands)
    moved += sum(math.prod(o.shape) * o.dtype.itemsize for o in jax.tree.leaves(out_shape))
    whole = pl.BlockSpec(memory_space=pltpu.VMEM)
    if steps is None:
        grid, in_blocks = (), [whole] * len(operands)
        out_blocks = out_blocks or jax.tree.map(lambda _: whole, out_shape)
    else:
        grid, in_blocks, out_blocks = (steps,), blocks[0], blocks[1]
    return pl.pallas_call(
        body,
        grid=grid,
        out_shape=out_shape,
        in_specs=[pl.BlockSpec(memory_space=pltpu.SMEM)] + in_blocks,
        out_specs=out_blocks,
        scratch_shapes=list(scratch),
        compiler_params=pltpu.CompilerParams(vmem_limit_bytes=14 * 1024 * 1024),
        cost_estimate=pl.CostEstimate(flops=flops, bytes_accessed=moved, transcendentals=0),
    )(role, *operands)


def block_at(shape, place):
    def index(step):
        return tuple(step if axis == place else 0 for axis in range(len(shape)))

    return pl.BlockSpec(shape, index)


def high_low(value):
    high = value.astype(bf16)
    return high, (value - high.astype(f32)).astype(bf16)


def partial_body(role, mine, in_inverse, out_inverse, out, ready, sems):
    deep = out_inverse.shape[1] // CORES

    def send(i):
        return pltpu.make_async_copy(ready.at[i], out.at[i], sems.at[i])

    @pl.when(role[0] == 0)
    def _():
        inverse = jnp.concatenate([in_inverse[0], in_inverse[1]], axis=1)

        @pl.loop(0, SIDE)
        def _(i):
            high, low = high_low(dot(flat(mine[i, :, 0]), inverse, by_cols))
            ready[i, 0] = high
            ready[i, 1] = low
            send(i).start()

    @pl.when(role[0] == 1)
    def _():
        @pl.loop(0, SIDE)
        def _(i):
            near, far = flat(mine[i, :, 0]), flat(mine[i, :, 1])
            for half in range(CORES):
                part = dot(near, out_inverse[half, :deep], plain)
                part = part + dot(far, out_inverse[half, deep:], plain)
                ready[i, half] = part.astype(bf16)
            send(i).start()

    @pl.loop(0, SIDE)
    def _(i):
        send(i).wait()


def resum(first, parts):
    total = jnp.sum(parts.astype(f32), axis=0)
    whole = total[0] + total[1]
    high = lax.reduce_precision(whole, exponent_bits=8, mantissa_bits=7)
    parts = [
        jnp.where(first, high, total[0]).astype(bf16),
        jnp.where(first, whole - high, total[1]).astype(bf16),
    ]
    return jnp.stack([part.reshape(SIDE, -1, part.shape[1]) for part in parts], axis=1)


def finish_body(role, parts, out):
    totals = [sum(parts[k, half].astype(f32) for k in range(SIDE)) for half in range(CORES)]

    @pl.when(role[0] == 0)
    def _():
        out[0] = (totals[0] + totals[1]).astype(bf16)
        out[1] = jnp.zeros_like(out[1])

    @pl.when(role[0] == 1)
    def _():
        out[0] = totals[0].astype(bf16)
        out[1] = totals[1].astype(bf16)


def natural_body(tokens, role, mixed, crossed, out):
    @pl.when(pl.program_id(0) == 0)
    def _():
        out[...] = jnp.zeros_like(out)

    @pl.when(role[0] == 0)
    def _():
        out[...] += dot(flat(mixed[0, :, 0]), flat(crossed[0]), by_rows) / tokens

    @pl.when(role[0] == 1)
    def _():
        out[...] += dot(flat(crossed[0]), flat(mixed[0, :, 1]), by_rows) / tokens


def running_body(role, mine, their, late, their_late, in_old, out_old, in_new, out_new):
    tokens = late.shape[0] * late.shape[1] * late.shape[2]
    width, wide = in_old.shape[1], out_old.shape[1]
    new_part = 1.0 - stat_decay

    def finish(in_rows, near_rows, far_rows, in_cols, out_cols):
        batch = sum(dot(in_rows(i), in_cols(i), by_rows) for i in range(SIDE)) / tokens
        in_new[...] = stat_decay * in_old[...] + new_part * batch
        for half, rows in ((0, near_rows), (1, far_rows)):
            at = pl.ds(half * wide, wide)
            batch = sum(dot(rows(i), out_cols(i), by_rows) for i in range(SIDE)) / tokens
            out_new[at, :] = stat_decay * out_old[at, :] + new_part * batch

    def part(ref, half, start=0, stop=None):
        return lambda i: flat(ref[i, :, half, :, start:stop])

    def turned(ref, spot):
        return lambda i: flat(ref[lax.rem(spot + (SIDE - i), SIDE)])

    @pl.when(role[0] == 0)
    def _():
        rows, cols = turned(their_late, role[2]), part(mine, 0, 0, width)
        finish(rows, part(their, 0), part(their, 1), cols, part(mine, 1))

    @pl.when(role[0] == 1)
    def _():
        rows, cols = turned(late, role[1]), part(their, 0, width)
        finish(rows, part(mine, 0), part(mine, 1), cols, turned(their_late, role[2]))


def per_device(
    layer_inputs, output_grads, input_factor, output_factor, input_inverse, output_inverse
):
    rows = layer_inputs.shape[0]
    wide = output_grads.shape[1]
    tokens = rows * SIDE * SIDE
    core = lax.axis_index("core")
    first = core == 0
    role = core.astype(jnp.int32).reshape(1)
    spot = (lax.axis_index("x"), lax.axis_index("y"))
    tied = lax.optimization_barrier

    out_z = role_groups("zh", "zl")
    out_xy = role_groups("x", "y")
    back_z = role_groups("zl", "zh")
    back_xy = role_groups("y", "x")

    grads_pair = lax.all_gather(output_grads, "core", axis=0, tiled=False)
    grads_moved = lax.ppermute(grads_pair, ALL, swap_pairs())
    grads_pair, layer_inputs = tied((grads_pair, layer_inputs))
    input_pair = lax.all_gather(layer_inputs, "core", axis=1, tiled=True)
    inputs_moved = lax.ppermute(input_pair, ALL, swap_pairs())
    block = jnp.where(first, jnp.stack([input_pair, grads_pair[0]]), grads_moved)
    block = gather(block, out_z)
    block, late, inputs_moved, input_inverse, output_inverse = tied(
        (block, grads_pair[1], inputs_moved, input_inverse, output_inverse)
    )
    mine = gather_direct(block, out_xy)
    in_inverse = lax.all_gather(input_inverse, "core", axis=0, tiled=False)
    out_inverse = lax.all_gather(output_inverse, "core", axis=0, tiled=False)

    part = local_call(
        partial_body,
        pltpu.HBM((SIDE, CORES, SIDE * rows, wide), bf16),
        role,
        mine,
        in_inverse,
        out_inverse,
        flops=2 * tokens * 4 * wide * wide,
        out_blocks=pl.BlockSpec(memory_space=pltpu.HBM),
        scratch=[
            pltpu.VMEM((SIDE, CORES, SIDE * rows, wide), bf16),
            pltpu.SemaphoreType.DMA((SIDE,)),
        ],
    )
    part, late = tied((part, late))
    late = gather(jnp.where(first, late, inputs_moved), out_z)
    part = exchange(part, back_xy)
    part, late = tied((part, late))
    part = resum(first, part)
    part, late = tied((part, late))
    part = exchange(part, back_z)
    left = lax.ppermute(late, ALL, ring_pairs(1))
    right = lax.ppermute(late, ALL, ring_pairs(-1))
    span = SIDE // CORES
    ahead = lax.ppermute(left[:span], ALL, ring_pairs(1))
    behind = lax.ppermute(right[span:], ALL, ring_pairs(-1))
    late = jnp.stack([late, left, jnp.concatenate([ahead, behind]), right])
    late, mine = tied((late, mine))
    their, their_late = core_swap(mine), core_swap(late)
    part, late = tied((part, late))
    mixed = local_call(
        finish_body, jax.ShapeDtypeStruct((CORES, rows, wide), bf16), role, part
    )
    mixed = gather(mixed, back_z)
    mixed = gather_direct(mixed, back_xy)
    input_running, output_running = local_call(
        running_body,
        (
            jax.ShapeDtypeStruct(input_factor.shape, f32),
            jax.ShapeDtypeStruct(output_factor.shape, f32),
        ),
        jnp.stack([core, jnp.where(first, spot[0], spot[1]), jnp.where(first, spot[1], spot[0])]),
        mine,
        their,
        late,
        their_late,
        input_factor,
        output_factor,
        flops=2 * tokens * (2 * wide * wide + wide * wide // 2),
    )
    mixed, input_running, output_running = tied((mixed, input_running, output_running))
    crossed = core_swap(mixed[:, :, 0])
    natural_gradient = local_call(
        functools.partial(natural_body, tokens),
        jax.ShapeDtypeStruct((wide, wide), f32),
        role,
        mixed,
        crossed,
        flops=2 * tokens * wide * wide,
        steps=SIDE,
        blocks=(
            [
                block_at((1, SIDE, CORES, rows, wide), 0),
                block_at((1, SIDE, rows, wide), 0),
            ],
            block_at((wide, wide), None),
        ),
    )
    return (input_running, output_running, natural_gradient)


def solution(mesh):
    grid = Mesh(mesh.devices.reshape(SIDE, SIDE, SIDE, SIDE, CORES), ALL)
    spec = P(TOK, FEAT)
    return jax.shard_map(
        per_device, mesh=grid, in_specs=(spec,) * 6, out_specs=(spec,) * 3, check_vma=False
    )
```

```python
import functools
import math

import jax
import jax.numpy as jnp
from jax import lax
from jax.experimental import pallas as pl
from jax.experimental.pallas import tpu as pltpu
from jax.sharding import Mesh, PartitionSpec as P

stat_decay = 0.9
by_rows = (((0,), (0,)), ((), ()))
by_cols = (((1,), (1,)), ((), ()))
plain = (((1,), (0,)), ((), ()))
TOK = ("x", "zh")
FEAT = ("y", "zl", "core")
ALL = TOK + FEAT
SIDE = 4
CORES = 2
f32, bf16 = jnp.float32, jnp.bfloat16


def device(x, zh, y, zl, core):
    return (((x * SIDE + zh) * SIDE + y) * SIDE + zl) * CORES + core


def role_groups(first, second):
    groups = []
    for core, axis in ((0, first), (1, second)):
        others = [name for name in ALL[:4] if name != axis]
        for i in range(SIDE):
            for j in range(SIDE):
                for k in range(SIDE):
                    fixed = dict(zip(others, (i, j, k)))
                    groups.append(
                        [device(core=core, **fixed, **{axis: n}) for n in range(SIDE)]
                    )
    return groups


def swap_pairs():
    pairs = []
    for x in range(SIDE):
        for zh in range(SIDE):
            for y in range(SIDE):
                for zl in range(SIDE):
                    pairs.append((device(x, zh, y, zl, 0), device(x, zh, y, zl, 0)))
                    pairs.append((device(x, zh, y, zl, 1), device(y, zl, x, zh, 1)))
    return pairs


def ring_pairs(turn):
    pairs = []
    for group in role_groups("x", "y"):
        pairs += [(group[n], group[(n + turn) % SIDE]) for n in range(SIDE)]
    return pairs


def gather(block, groups):
    return lax.all_gather(block, ALL, axis_index_groups=groups, axis=0, tiled=False)


def exchange(parts, groups):
    return lax.all_to_all(parts, ALL, 0, 0, axis_index_groups=groups)


def gather_direct(block, groups):
    return exchange(jnp.broadcast_to(block[None], (SIDE,) + block.shape), groups)


def core_swap(block):
    return lax.ppermute(block, "core", [(0, 1), (1, 0)])


def dot(left, right, dims):
    return lax.dot_general(left, right, dims, preferred_element_type=f32)


def flat(block):
    return block.reshape(-1, block.shape[-1])


def local_call(body, out_shape, role, *operands, flops=0, steps=None, blocks=None, out_blocks=None, scratch=()):
    moved = sum(o.size * o.dtype.itemsize for o in operands)
    moved += sum(math.prod(o.shape) * o.dtype.itemsize for o in jax.tree.leaves(out_shape))
    whole = pl.BlockSpec(memory_space=pltpu.VMEM)
    if steps is None:
        grid, in_blocks = (), [whole] * len(operands)
        out_blocks = out_blocks or jax.tree.map(lambda _: whole, out_shape)
    else:
        grid, in_blocks, out_blocks = (steps,), blocks[0], blocks[1]
    return pl.pallas_call(
        body,
        grid=grid,
        out_shape=out_shape,
        in_specs=[pl.BlockSpec(memory_space=pltpu.SMEM)] + in_blocks,
        out_specs=out_blocks,
        scratch_shapes=list(scratch),
        compiler_params=pltpu.CompilerParams(vmem_limit_bytes=14 * 1024 * 1024),
        cost_estimate=pl.CostEstimate(flops=flops, bytes_accessed=moved, transcendentals=0),
    )(role, *operands)


def block_at(shape, place):
    def index(step):
        return tuple(step if axis == place else 0 for axis in range(len(shape)))

    return pl.BlockSpec(shape, index)


def high_low(value):
    high = value.astype(bf16)
    return high, (value - high.astype(f32)).astype(bf16)


def partial_body(role, mine, in_inverse, out_inverse, out, ready, sems):
    deep = out_inverse.shape[1] // CORES

    def send(i):
        return pltpu.make_async_copy(ready.at[i], out.at[i], sems.at[i])

    @pl.when(role[0] == 0)
    def _():
        inverse = jnp.concatenate([in_inverse[0], in_inverse[1]], axis=1)

        @pl.loop(0, SIDE)
        def _(i):
            high, low = high_low(dot(flat(mine[i, :, 0]), inverse, by_cols))
            ready[i, 0] = high
            ready[i, 1] = low
            send(i).start()

    @pl.when(role[0] == 1)
    def _():
        @pl.loop(0, SIDE)
        def _(i):
            near, far = flat(mine[i, :, 0]), flat(mine[i, :, 1])
            for half in range(CORES):
                part = dot(near, out_inverse[half, :deep], plain)
                part = part + dot(far, out_inverse[half, deep:], plain)
                ready[i, half] = part.astype(bf16)
            send(i).start()

    @pl.loop(0, SIDE)
    def _(i):
        send(i).wait()


def resum(first, parts):
    total = jnp.sum(parts.astype(f32), axis=0)
    whole = total[0] + total[1]
    high = lax.reduce_precision(whole, exponent_bits=8, mantissa_bits=7)
    parts = [
        jnp.where(first, high, total[0]).astype(bf16),
        jnp.where(first, whole - high, total[1]).astype(bf16),
    ]
    return jnp.stack([part.reshape(SIDE, -1, part.shape[1]) for part in parts], axis=1)


def finish_body(role, parts, out):
    totals = [sum(parts[k, half].astype(f32) for k in range(SIDE)) for half in range(CORES)]

    @pl.when(role[0] == 0)
    def _():
        out[0] = (totals[0] + totals[1]).astype(bf16)
        out[1] = jnp.zeros_like(out[1])

    @pl.when(role[0] == 1)
    def _():
        out[0] = totals[0].astype(bf16)
        out[1] = totals[1].astype(bf16)


def natural_body(tokens, role, mixed, crossed, out):
    @pl.when(pl.program_id(0) == 0)
    def _():
        out[...] = jnp.zeros_like(out)

    @pl.when(role[0] == 0)
    def _():
        out[...] += dot(flat(mixed[0, :, 0]), flat(crossed[0]), by_rows) / tokens

    @pl.when(role[0] == 1)
    def _():
        out[...] += dot(flat(crossed[0]), flat(mixed[0, :, 1]), by_rows) / tokens


def running_body(role, mine, their, late, their_late, in_old, out_old, in_new, out_new):
    tokens = late.shape[0] * late.shape[1] * late.shape[2]
    width, wide = in_old.shape[1], out_old.shape[1]
    new_part = 1.0 - stat_decay

    def finish(in_rows, near_rows, far_rows, in_cols, out_cols):
        batch = sum(dot(in_rows(i), in_cols(i), by_rows) for i in range(SIDE)) / tokens
        in_new[...] = stat_decay * in_old[...] + new_part * batch
        for half, rows in ((0, near_rows), (1, far_rows)):
            at = pl.ds(half * wide, wide)
            batch = sum(dot(rows(i), out_cols(i), by_rows) for i in range(SIDE)) / tokens
            out_new[at, :] = stat_decay * out_old[at, :] + new_part * batch

    def part(ref, half, start=0, stop=None):
        return lambda i: flat(ref[i, :, half, :, start:stop])

    def turned(ref, spot):
        return lambda i: flat(ref[lax.rem(spot + (SIDE - i), SIDE)])

    @pl.when(role[0] == 0)
    def _():
        rows, cols = turned(their_late, role[2]), part(mine, 0, 0, width)
        finish(rows, part(their, 0), part(their, 1), cols, part(mine, 1))

    @pl.when(role[0] == 1)
    def _():
        rows, cols = turned(late, role[1]), part(their, 0, width)
        finish(rows, part(mine, 0), part(mine, 1), cols, turned(their_late, role[2]))


def per_device(
    layer_inputs, output_grads, input_factor, output_factor, input_inverse, output_inverse
):
    rows = layer_inputs.shape[0]
    wide = output_grads.shape[1]
    tokens = rows * SIDE * SIDE
    core = lax.axis_index("core")
    first = core == 0
    role = core.astype(jnp.int32).reshape(1)
    spot = (lax.axis_index("x"), lax.axis_index("y"))
    tied = lax.optimization_barrier

    out_z = role_groups("zh", "zl")
    out_xy = role_groups("x", "y")
    back_z = role_groups("zl", "zh")
    back_xy = role_groups("y", "x")

    grads_pair = lax.all_gather(output_grads, "core", axis=0, tiled=False)
    grads_moved = lax.ppermute(grads_pair, ALL, swap_pairs())
    grads_pair, layer_inputs = tied((grads_pair, layer_inputs))
    input_pair = lax.all_gather(layer_inputs, "core", axis=1, tiled=True)
    inputs_moved = lax.ppermute(input_pair, ALL, swap_pairs())
    block = jnp.where(first, jnp.stack([input_pair, grads_pair[0]]), grads_moved)
    block = gather(block, out_z)
    block, late, inputs_moved, input_inverse, output_inverse = tied(
        (block, grads_pair[1], inputs_moved, input_inverse, output_inverse)
    )
    mine = gather_direct(block, out_xy)
    in_inverse = lax.all_gather(input_inverse, "core", axis=0, tiled=False)
    out_inverse = lax.all_gather(output_inverse, "core", axis=0, tiled=False)

    part = local_call(
        partial_body,
        pltpu.HBM((SIDE, CORES, SIDE * rows, wide), bf16),
        role,
        mine,
        in_inverse,
        out_inverse,
        flops=2 * tokens * 4 * wide * wide,
        out_blocks=pl.BlockSpec(memory_space=pltpu.HBM),
        scratch=[
            pltpu.VMEM((SIDE, CORES, SIDE * rows, wide), bf16),
            pltpu.SemaphoreType.DMA((SIDE,)),
        ],
    )
    part, late, mine = tied((part, late, mine))
    their = core_swap(mine)
    late = gather(jnp.where(first, late, inputs_moved), out_z)
    part = exchange(part, back_xy)
    part, late = tied((part, late))
    part = resum(first, part)
    part, late = tied((part, late))
    part = exchange(part, back_z)
    left = lax.ppermute(late, ALL, ring_pairs(1))
    right = lax.ppermute(late, ALL, ring_pairs(-1))
    span = SIDE // CORES
    ahead = lax.ppermute(left[:span], ALL, ring_pairs(1))
    behind = lax.ppermute(right[span:], ALL, ring_pairs(-1))
    late = jnp.stack([late, left, jnp.concatenate([ahead, behind]), right])
    their_late = core_swap(late)
    part, late = tied((part, late))
    mixed = local_call(
        finish_body, jax.ShapeDtypeStruct((CORES, rows, wide), bf16), role, part
    )
    mixed = gather(mixed, back_z)
    mixed = gather_direct(mixed, back_xy)
    input_running, output_running = local_call(
        running_body,
        (
            jax.ShapeDtypeStruct(input_factor.shape, f32),
            jax.ShapeDtypeStruct(output_factor.shape, f32),
        ),
        jnp.stack([core, jnp.where(first, spot[0], spot[1]), jnp.where(first, spot[1], spot[0])]),
        mine,
        their,
        late,
        their_late,
        input_factor,
        output_factor,
        flops=2 * tokens * (2 * wide * wide + wide * wide // 2),
    )
    mixed, input_running, output_running = tied((mixed, input_running, output_running))
    crossed = core_swap(mixed[:, :, 0])
    natural_gradient = local_call(
        functools.partial(natural_body, tokens),
        jax.ShapeDtypeStruct((wide, wide), f32),
        role,
        mixed,
        crossed,
        flops=2 * tokens * wide * wide,
        steps=SIDE,
        blocks=(
            [
                block_at((1, SIDE, CORES, rows, wide), 0),
                block_at((1, SIDE, rows, wide), 0),
            ],
            block_at((wide, wide), None),
        ),
    )
    return (input_running, output_running, natural_gradient)


def solution(mesh):
    grid = Mesh(mesh.devices.reshape(SIDE, SIDE, SIDE, SIDE, CORES), ALL)
    spec = P(TOK, FEAT)
    return jax.shard_map(
        per_device, mesh=grid, in_specs=(spec,) * 6, out_specs=(spec,) * 3, check_vma=False
    )
```

```python
import functools
import math

import jax
import jax.numpy as jnp
from jax import lax
from jax.experimental import pallas as pl
from jax.experimental.pallas import tpu as pltpu
from jax.sharding import Mesh, PartitionSpec as P

stat_decay = 0.9
by_rows = (((0,), (0,)), ((), ()))
by_cols = (((1,), (1,)), ((), ()))
plain = (((1,), (0,)), ((), ()))
TOK = ("x", "zh")
FEAT = ("y", "zl", "core")
ALL = TOK + FEAT
SIDE = 4
CORES = 2
f32, bf16 = jnp.float32, jnp.bfloat16


def device(x, zh, y, zl, core):
    return (((x * SIDE + zh) * SIDE + y) * SIDE + zl) * CORES + core


def role_groups(first, second):
    groups = []
    for core, axis in ((0, first), (1, second)):
        others = [name for name in ALL[:4] if name != axis]
        for i in range(SIDE):
            for j in range(SIDE):
                for k in range(SIDE):
                    fixed = dict(zip(others, (i, j, k)))
                    groups.append(
                        [device(core=core, **fixed, **{axis: n}) for n in range(SIDE)]
                    )
    return groups


def swap_pairs():
    pairs = []
    for x in range(SIDE):
        for zh in range(SIDE):
            for y in range(SIDE):
                for zl in range(SIDE):
                    pairs.append((device(x, zh, y, zl, 0), device(x, zh, y, zl, 0)))
                    pairs.append((device(x, zh, y, zl, 1), device(y, zl, x, zh, 1)))
    return pairs


def ring_pairs(turn):
    pairs = []
    for group in role_groups("x", "y"):
        pairs += [(group[n], group[(n + turn) % SIDE]) for n in range(SIDE)]
    return pairs


def gather(block, groups):
    return lax.all_gather(block, ALL, axis_index_groups=groups, axis=0, tiled=False)


def exchange(parts, groups):
    return lax.all_to_all(parts, ALL, 0, 0, axis_index_groups=groups)


def gather_direct(block, groups):
    return exchange(jnp.broadcast_to(block[None], (SIDE,) + block.shape), groups)


def core_swap(block):
    return lax.ppermute(block, "core", [(0, 1), (1, 0)])


def dot(left, right, dims):
    return lax.dot_general(left, right, dims, preferred_element_type=f32)


def flat(block):
    return block.reshape(-1, block.shape[-1])


def local_call(body, out_shape, role, *operands, flops=0, steps=None, blocks=None, out_blocks=None, scratch=()):
    moved = sum(o.size * o.dtype.itemsize for o in operands)
    moved += sum(math.prod(o.shape) * o.dtype.itemsize for o in jax.tree.leaves(out_shape))
    whole = pl.BlockSpec(memory_space=pltpu.VMEM)
    if steps is None:
        grid, in_blocks = (), [whole] * len(operands)
        out_blocks = out_blocks or jax.tree.map(lambda _: whole, out_shape)
    else:
        grid, in_blocks, out_blocks = (steps,), blocks[0], blocks[1]
    return pl.pallas_call(
        body,
        grid=grid,
        out_shape=out_shape,
        in_specs=[pl.BlockSpec(memory_space=pltpu.SMEM)] + in_blocks,
        out_specs=out_blocks,
        scratch_shapes=list(scratch),
        compiler_params=pltpu.CompilerParams(vmem_limit_bytes=14 * 1024 * 1024),
        cost_estimate=pl.CostEstimate(flops=flops, bytes_accessed=moved, transcendentals=0),
    )(role, *operands)


def block_at(shape, place):
    def index(step):
        return tuple(step if axis == place else 0 for axis in range(len(shape)))

    return pl.BlockSpec(shape, index)


def high_low(value):
    high = value.astype(bf16)
    return high, (value - high.astype(f32)).astype(bf16)


def partial_body(role, mine, in_inverse, out_inverse, out, ready, sems):
    deep = out_inverse.shape[1] // CORES

    def send(i):
        return pltpu.make_async_copy(ready.at[i], out.at[i], sems.at[i])

    @pl.when(role[0] == 0)
    def _():
        inverse = jnp.concatenate([in_inverse[0], in_inverse[1]], axis=1)

        @pl.loop(0, SIDE)
        def _(i):
            high, low = high_low(dot(flat(mine[i, :, 0]), inverse, by_cols))
            ready[i, 0] = high
            ready[i, 1] = low
            send(i).start()

    @pl.when(role[0] == 1)
    def _():
        @pl.loop(0, SIDE)
        def _(i):
            near, far = flat(mine[i, :, 0]), flat(mine[i, :, 1])
            for half in range(CORES):
                part = dot(near, out_inverse[half, :deep], plain)
                part = part + dot(far, out_inverse[half, deep:], plain)
                ready[i, half] = part.astype(bf16)
            send(i).start()

    @pl.loop(0, SIDE)
    def _(i):
        send(i).wait()


def resum(first, parts):
    total = jnp.sum(parts.astype(f32), axis=0)
    whole = total[0] + total[1]
    high = lax.reduce_precision(whole, exponent_bits=8, mantissa_bits=7)
    parts = [
        jnp.where(first, high, total[0]).astype(bf16),
        jnp.where(first, whole - high, total[1]).astype(bf16),
    ]
    return jnp.stack([part.reshape(SIDE, -1, part.shape[1]) for part in parts], axis=1)


def finish_body(role, parts, out):
    totals = [sum(parts[k, half].astype(f32) for k in range(SIDE)) for half in range(CORES)]

    @pl.when(role[0] == 0)
    def _():
        out[0] = (totals[0] + totals[1]).astype(bf16)
        out[1] = jnp.zeros_like(out[1])

    @pl.when(role[0] == 1)
    def _():
        out[0] = totals[0].astype(bf16)
        out[1] = totals[1].astype(bf16)


def natural_body(tokens, role, mixed, crossed, out):
    @pl.when(pl.program_id(0) == 0)
    def _():
        out[...] = jnp.zeros_like(out)

    @pl.when(role[0] == 0)
    def _():
        out[...] += dot(flat(mixed[0, :, 0]), flat(crossed[0]), by_rows) / tokens

    @pl.when(role[0] == 1)
    def _():
        out[...] += dot(flat(crossed[0]), flat(mixed[0, :, 1]), by_rows) / tokens


def running_body(role, mine, their, late, their_late, in_old, out_old, in_new, out_new):
    tokens = late.shape[0] * late.shape[1] * late.shape[2]
    width, wide = in_old.shape[1], out_old.shape[1]
    new_part = 1.0 - stat_decay

    def finish(in_rows, near_rows, far_rows, in_cols, out_cols):
        batch = sum(dot(in_rows(i), in_cols(i), by_rows) for i in range(SIDE)) / tokens
        in_new[...] = stat_decay * in_old[...] + new_part * batch
        for half, rows in ((0, near_rows), (1, far_rows)):
            at = pl.ds(half * wide, wide)
            batch = sum(dot(rows(i), out_cols(i), by_rows) for i in range(SIDE)) / tokens
            out_new[at, :] = stat_decay * out_old[at, :] + new_part * batch

    def part(ref, half, start=0, stop=None):
        return lambda i: flat(ref[i, :, half, :, start:stop])

    def turned(ref, spot):
        return lambda i: flat(ref[lax.rem(spot + (SIDE - i), SIDE)])

    @pl.when(role[0] == 0)
    def _():
        rows, cols = turned(their_late, role[2]), part(mine, 0, 0, width)
        finish(rows, part(their, 0), part(their, 1), cols, part(mine, 1))

    @pl.when(role[0] == 1)
    def _():
        rows, cols = turned(late, role[1]), part(their, 0, width)
        finish(rows, part(mine, 0), part(mine, 1), cols, turned(their_late, role[2]))


def per_device(
    layer_inputs, output_grads, input_factor, output_factor, input_inverse, output_inverse
):
    rows = layer_inputs.shape[0]
    wide = output_grads.shape[1]
    tokens = rows * SIDE * SIDE
    core = lax.axis_index("core")
    first = core == 0
    role = core.astype(jnp.int32).reshape(1)
    spot = (lax.axis_index("x"), lax.axis_index("y"))
    tied = lax.optimization_barrier

    out_z = role_groups("zh", "zl")
    out_xy = role_groups("x", "y")
    back_z = role_groups("zl", "zh")
    back_xy = role_groups("y", "x")

    grads_pair = lax.all_gather(output_grads, "core", axis=0, tiled=False)
    grads_moved = lax.ppermute(grads_pair, ALL, swap_pairs())
    grads_pair, layer_inputs = tied((grads_pair, layer_inputs))
    input_pair = lax.all_gather(layer_inputs, "core", axis=1, tiled=True)
    inputs_moved = lax.ppermute(input_pair, ALL, swap_pairs())
    block = jnp.where(first, jnp.stack([input_pair, grads_pair[0]]), grads_moved)
    block = gather(block, out_z)
    block, late, inputs_moved, input_inverse, output_inverse = tied(
        (block, grads_pair[1], inputs_moved, input_inverse, output_inverse)
    )
    mine = gather_direct(block, out_xy)
    in_inverse = lax.all_gather(input_inverse, "core", axis=0, tiled=False)
    out_inverse = lax.all_gather(output_inverse, "core", axis=0, tiled=False)

    part = local_call(
        partial_body,
        pltpu.HBM((SIDE, CORES, SIDE * rows, wide), bf16),
        role,
        mine,
        in_inverse,
        out_inverse,
        flops=2 * tokens * 4 * wide * wide,
        out_blocks=pl.BlockSpec(memory_space=pltpu.HBM),
        scratch=[
            pltpu.VMEM((SIDE, CORES, SIDE * rows, wide), bf16),
            pltpu.SemaphoreType.DMA((SIDE,)),
        ],
    )
    part, late, mine = tied((part, late, mine))
    their = core_swap(mine)
    late = gather(jnp.where(first, late, inputs_moved), out_z)
    part = exchange(part, back_xy)
    part, late = tied((part, late))
    part = resum(first, part)
    part, late = tied((part, late))
    part = exchange(part, back_z)
    turns = [lax.ppermute(late, ALL, ring_pairs(turn)) for turn in range(1, SIDE)]
    late = jnp.stack([late] + turns)
    their_late = core_swap(late)
    part, late = tied((part, late))
    mixed = local_call(
        finish_body, jax.ShapeDtypeStruct((CORES, rows, wide), bf16), role, part
    )
    mixed = gather(mixed, back_z)
    mixed = gather_direct(mixed, back_xy)
    input_running, output_running = local_call(
        running_body,
        (
            jax.ShapeDtypeStruct(input_factor.shape, f32),
            jax.ShapeDtypeStruct(output_factor.shape, f32),
        ),
        jnp.stack([core, jnp.where(first, spot[0], spot[1]), jnp.where(first, spot[1], spot[0])]),
        mine,
        their,
        late,
        their_late,
        input_factor,
        output_factor,
        flops=2 * tokens * (2 * wide * wide + wide * wide // 2),
    )
    mixed, input_running, output_running = tied((mixed, input_running, output_running))
    crossed = core_swap(mixed[:, :, 0])
    natural_gradient = local_call(
        functools.partial(natural_body, tokens),
        jax.ShapeDtypeStruct((wide, wide), f32),
        role,
        mixed,
        crossed,
        flops=2 * tokens * wide * wide,
        steps=SIDE,
        blocks=(
            [
                block_at((1, SIDE, CORES, rows, wide), 0),
                block_at((1, SIDE, rows, wide), 0),
            ],
            block_at((wide, wide), None),
        ),
    )
    return (input_running, output_running, natural_gradient)


def solution(mesh):
    grid = Mesh(mesh.devices.reshape(SIDE, SIDE, SIDE, SIDE, CORES), ALL)
    spec = P(TOK, FEAT)
    return jax.shard_map(
        per_device, mesh=grid, in_specs=(spec,) * 6, out_specs=(spec,) * 3, check_vma=False
    )
```

```python
import functools
import math

import jax
import jax.numpy as jnp
from jax import lax
from jax.experimental import pallas as pl
from jax.experimental.pallas import tpu as pltpu
from jax.sharding import Mesh, PartitionSpec as P

stat_decay = 0.9
by_rows = (((0,), (0,)), ((), ()))
by_cols = (((1,), (1,)), ((), ()))
plain = (((1,), (0,)), ((), ()))
TOK = ("x", "zh")
FEAT = ("y", "zl", "core")
ALL = TOK + FEAT
SIDE = 4
CORES = 2
f32, bf16 = jnp.float32, jnp.bfloat16


def device(x, zh, y, zl, core):
    return (((x * SIDE + zh) * SIDE + y) * SIDE + zl) * CORES + core


def role_groups(first, second):
    groups = []
    for core, axis in ((0, first), (1, second)):
        others = [name for name in ALL[:4] if name != axis]
        for i in range(SIDE):
            for j in range(SIDE):
                for k in range(SIDE):
                    fixed = dict(zip(others, (i, j, k)))
                    groups.append(
                        [device(core=core, **fixed, **{axis: n}) for n in range(SIDE)]
                    )
    return groups


def swap_pairs():
    pairs = []
    for x in range(SIDE):
        for zh in range(SIDE):
            for y in range(SIDE):
                for zl in range(SIDE):
                    pairs.append((device(x, zh, y, zl, 0), device(x, zh, y, zl, 0)))
                    pairs.append((device(x, zh, y, zl, 1), device(y, zl, x, zh, 1)))
    return pairs


def ring_pairs(turn):
    pairs = []
    for group in role_groups("x", "y"):
        pairs += [(group[n], group[(n + turn) % SIDE]) for n in range(SIDE)]
    return pairs


def gather(block, groups):
    return lax.all_gather(block, ALL, axis_index_groups=groups, axis=0, tiled=False)


def exchange(parts, groups):
    return lax.all_to_all(parts, ALL, 0, 0, axis_index_groups=groups)


def gather_direct(block, groups):
    return exchange(jnp.broadcast_to(block[None], (SIDE,) + block.shape), groups)


def core_swap(block):
    return lax.ppermute(block, "core", [(0, 1), (1, 0)])


def dot(left, right, dims):
    return lax.dot_general(left, right, dims, preferred_element_type=f32)


def flat(block):
    return block.reshape(-1, block.shape[-1])


def local_call(body, out_shape, role, *operands, flops=0, steps=None, blocks=None, out_blocks=None, scratch=()):
    moved = sum(o.size * o.dtype.itemsize for o in operands)
    moved += sum(math.prod(o.shape) * o.dtype.itemsize for o in jax.tree.leaves(out_shape))
    whole = pl.BlockSpec(memory_space=pltpu.VMEM)
    if steps is None:
        grid, in_blocks = (), [whole] * len(operands)
        out_blocks = out_blocks or jax.tree.map(lambda _: whole, out_shape)
    else:
        grid, in_blocks, out_blocks = (steps,), blocks[0], blocks[1]
    return pl.pallas_call(
        body,
        grid=grid,
        out_shape=out_shape,
        in_specs=[pl.BlockSpec(memory_space=pltpu.SMEM)] + in_blocks,
        out_specs=out_blocks,
        scratch_shapes=list(scratch),
        compiler_params=pltpu.CompilerParams(vmem_limit_bytes=14 * 1024 * 1024),
        cost_estimate=pl.CostEstimate(flops=flops, bytes_accessed=moved, transcendentals=0),
    )(role, *operands)


def block_at(shape, place):
    def index(step):
        return tuple(step if axis == place else 0 for axis in range(len(shape)))

    return pl.BlockSpec(shape, index)


def high_low(value):
    high = value.astype(bf16)
    return high, (value - high.astype(f32)).astype(bf16)


def partial_body(role, mine, in_inverse, out_own, other, out):
    deep = out_own.shape[0] // CORES

    @pl.when(role[0] == 0)
    def _():

        @pl.loop(0, SIDE)
        def _(i):
            high, low = high_low(dot(flat(mine[i, :, 0]), in_inverse[...], by_cols))
            out[i, 0] = high
            out[i, 1] = low

    @pl.when(role[0] == 1)
    def _():
        @pl.loop(0, SIDE)
        def _(i):
            near, far = flat(mine[i, :, 0]), flat(mine[i, :, 1])
            for half, inverse in ((0, other), (1, out_own)):
                part = dot(near, inverse[:deep], plain) + dot(far, inverse[deep:], plain)
                out[i, half] = part.astype(bf16)


def resum(first, parts):
    total = jnp.sum(parts.astype(f32), axis=0)
    whole = total[0] + total[1]
    high = lax.reduce_precision(whole, exponent_bits=8, mantissa_bits=7)
    parts = [
        jnp.where(first, high, total[0]).astype(bf16),
        jnp.where(first, whole - high, total[1]).astype(bf16),
    ]
    return jnp.stack([part.reshape(SIDE, -1, part.shape[1]) for part in parts], axis=1)


def finish_body(role, parts, out):
    totals = [sum(parts[k, half].astype(f32) for k in range(SIDE)) for half in range(CORES)]

    @pl.when(role[0] == 0)
    def _():
        out[0] = (totals[0] + totals[1]).astype(bf16)
        out[1] = jnp.zeros_like(out[1])

    @pl.when(role[0] == 1)
    def _():
        out[0] = totals[0].astype(bf16)
        out[1] = totals[1].astype(bf16)


def natural_body(tokens, role, mixed, crossed, out):
    @pl.when(pl.program_id(0) == 0)
    def _():
        out[...] = jnp.zeros_like(out)

    @pl.when(role[0] == 0)
    def _():
        out[...] += dot(flat(mixed[0, :, 0]), flat(crossed[0]), by_rows) / tokens

    @pl.when(role[0] == 1)
    def _():
        out[...] += dot(flat(crossed[0]), flat(mixed[0, :, 1]), by_rows) / tokens


def running_body(role, mine, their, late, their_late, in_old, out_old, in_new, out_new):
    tokens = late.shape[0] * late.shape[1] * late.shape[2]
    width, wide = in_old.shape[1], out_old.shape[1]
    new_part = 1.0 - stat_decay

    def finish(in_rows, near_rows, far_rows, in_cols, out_cols):
        batch = sum(dot(in_rows(i), in_cols(i), by_rows) for i in range(SIDE)) / tokens
        in_new[...] = stat_decay * in_old[...] + new_part * batch
        for half, rows in ((0, near_rows), (1, far_rows)):
            at = pl.ds(half * wide, wide)
            batch = sum(dot(rows(i), out_cols(i), by_rows) for i in range(SIDE)) / tokens
            out_new[at, :] = stat_decay * out_old[at, :] + new_part * batch

    def part(ref, half, start=0, stop=None):
        return lambda i: flat(ref[i, :, half, :, start:stop])

    def turned(ref, spot):
        return lambda i: flat(ref[lax.rem(spot + (SIDE - i), SIDE)])

    @pl.when(role[0] == 0)
    def _():
        rows, cols = turned(their_late, role[2]), part(mine, 0, 0, width)
        finish(rows, part(their, 0), part(their, 1), cols, part(mine, 1))

    @pl.when(role[0] == 1)
    def _():
        rows, cols = turned(late, role[1]), part(their, 0, width)
        finish(rows, part(mine, 0), part(mine, 1), cols, turned(their_late, role[2]))


def per_device(
    layer_inputs, output_grads, input_factor, output_factor, input_inverse, output_inverse
):
    rows = layer_inputs.shape[0]
    wide = output_grads.shape[1]
    tokens = rows * SIDE * SIDE
    core = lax.axis_index("core")
    first = core == 0
    role = core.astype(jnp.int32).reshape(1)
    spot = (lax.axis_index("x"), lax.axis_index("y"))
    tied = lax.optimization_barrier

    out_z = role_groups("zh", "zl")
    out_xy = role_groups("x", "y")
    back_z = role_groups("zl", "zh")
    back_xy = role_groups("y", "x")

    grads_pair = lax.all_gather(output_grads, "core", axis=0, tiled=False)
    grads_moved = lax.ppermute(grads_pair, ALL, swap_pairs())
    grads_pair, layer_inputs, input_inverse = tied((grads_pair, layer_inputs, input_inverse))
    input_pair = jnp.concatenate([layer_inputs, input_inverse])
    input_pair = lax.all_gather(input_pair, "core", axis=1, tiled=True)
    input_pair, in_inverse = input_pair[:rows], input_pair[rows:]
    inputs_moved = lax.ppermute(input_pair, ALL, swap_pairs())
    block = jnp.where(first, jnp.stack([input_pair, grads_pair[0]]), grads_moved)
    block = gather(block, out_z)
    block, late, inputs_moved, other = tied(
        (block, grads_pair[1], inputs_moved, output_inverse)
    )
    mine = gather_direct(block, out_xy)
    other = core_swap(other)
    late = gather(jnp.where(first, late, inputs_moved), out_z)
    mine, late = tied((mine, late))

    part = local_call(
        partial_body,
        jax.ShapeDtypeStruct((SIDE, CORES, SIDE * rows, wide), bf16),
        role,
        mine,
        in_inverse,
        output_inverse,
        other,
        flops=2 * tokens * 4 * wide * wide,
    )
    part = exchange(part, back_xy)
    part = resum(first, part)
    part, late, mine = tied((part, late, mine))
    their = core_swap(mine)
    part = exchange(part, back_z)
    turns = [lax.ppermute(late, ALL, ring_pairs(turn)) for turn in range(1, SIDE)]
    late = jnp.stack([late] + turns)
    their_late = core_swap(late)
    part, late = tied((part, late))
    mixed = local_call(
        finish_body, jax.ShapeDtypeStruct((CORES, rows, wide), bf16), role, part
    )
    mixed = gather(mixed, back_z)
    mixed = gather_direct(mixed, back_xy)
    input_running, output_running = local_call(
        running_body,
        (
            jax.ShapeDtypeStruct(input_factor.shape, f32),
            jax.ShapeDtypeStruct(output_factor.shape, f32),
        ),
        jnp.stack([core, jnp.where(first, spot[0], spot[1]), jnp.where(first, spot[1], spot[0])]),
        mine,
        their,
        late,
        their_late,
        input_factor,
        output_factor,
        flops=2 * tokens * (2 * wide * wide + wide * wide // 2),
    )
    mixed, input_running, output_running = tied((mixed, input_running, output_running))
    crossed = core_swap(mixed[:, :, 0])
    natural_gradient = local_call(
        functools.partial(natural_body, tokens),
        jax.ShapeDtypeStruct((wide, wide), f32),
        role,
        mixed,
        crossed,
        flops=2 * tokens * wide * wide,
        steps=SIDE,
        blocks=(
            [
                block_at((1, SIDE, CORES, rows, wide), 0),
                block_at((1, SIDE, rows, wide), 0),
            ],
            block_at((wide, wide), None),
        ),
    )
    return (input_running, output_running, natural_gradient)


def solution(mesh):
    grid = Mesh(mesh.devices.reshape(SIDE, SIDE, SIDE, SIDE, CORES), ALL)
    spec = P(TOK, FEAT)
    return jax.shard_map(
        per_device, mesh=grid, in_specs=(spec,) * 6, out_specs=(spec,) * 3, check_vma=False
    )
```

```python
import functools
import math

import jax
import jax.numpy as jnp
from jax import lax
from jax.experimental import pallas as pl
from jax.experimental.pallas import tpu as pltpu
from jax.sharding import Mesh, PartitionSpec as P

stat_decay = 0.9
by_rows = (((0,), (0,)), ((), ()))
by_cols = (((1,), (1,)), ((), ()))
plain = (((1,), (0,)), ((), ()))
TOK = ("x", "zh")
FEAT = ("y", "zl", "core")
ALL = TOK + FEAT
SIDE = 4
CORES = 2
f32, bf16 = jnp.float32, jnp.bfloat16


def device(x, zh, y, zl, core):
    return (((x * SIDE + zh) * SIDE + y) * SIDE + zl) * CORES + core


def role_groups(first, second):
    groups = []
    for core, axis in ((0, first), (1, second)):
        others = [name for name in ALL[:4] if name != axis]
        for i in range(SIDE):
            for j in range(SIDE):
                for k in range(SIDE):
                    fixed = dict(zip(others, (i, j, k)))
                    groups.append(
                        [device(core=core, **fixed, **{axis: n}) for n in range(SIDE)]
                    )
    return groups


def swap_pairs():
    pairs = []
    for x in range(SIDE):
        for zh in range(SIDE):
            for y in range(SIDE):
                for zl in range(SIDE):
                    pairs.append((device(x, zh, y, zl, 0), device(x, zh, y, zl, 0)))
                    pairs.append((device(x, zh, y, zl, 1), device(y, zl, x, zh, 1)))
    return pairs


def ring_pairs(turn):
    pairs = []
    for group in role_groups("x", "y"):
        pairs += [(group[n], group[(n + turn) % SIDE]) for n in range(SIDE)]
    return pairs


def gather(block, groups):
    return lax.all_gather(block, ALL, axis_index_groups=groups, axis=0, tiled=False)


def exchange(parts, groups):
    return lax.all_to_all(parts, ALL, 0, 0, axis_index_groups=groups)


def gather_direct(block, groups):
    return exchange(jnp.broadcast_to(block[None], (SIDE,) + block.shape), groups)


def core_swap(block):
    return lax.ppermute(block, "core", [(0, 1), (1, 0)])


def dot(left, right, dims):
    return lax.dot_general(left, right, dims, preferred_element_type=f32)


def flat(block):
    return block.reshape(-1, block.shape[-1])


def local_call(body, out_shape, role, *operands, flops=0, steps=None, blocks=None, out_blocks=None, scratch=()):
    moved = sum(o.size * o.dtype.itemsize for o in operands)
    moved += sum(math.prod(o.shape) * o.dtype.itemsize for o in jax.tree.leaves(out_shape))
    whole = pl.BlockSpec(memory_space=pltpu.VMEM)
    if steps is None:
        grid, in_blocks = (), [whole] * len(operands)
        out_blocks = out_blocks or jax.tree.map(lambda _: whole, out_shape)
    else:
        grid, in_blocks, out_blocks = (steps,), blocks[0], blocks[1]
    return pl.pallas_call(
        body,
        grid=grid,
        out_shape=out_shape,
        in_specs=[pl.BlockSpec(memory_space=pltpu.SMEM)] + in_blocks,
        out_specs=out_blocks,
        scratch_shapes=list(scratch),
        compiler_params=pltpu.CompilerParams(vmem_limit_bytes=14 * 1024 * 1024),
        cost_estimate=pl.CostEstimate(flops=flops, bytes_accessed=moved, transcendentals=0),
    )(role, *operands)


def block_at(shape, place):
    def index(step):
        return tuple(step if axis == place else 0 for axis in range(len(shape)))

    return pl.BlockSpec(shape, index)


def high_low(value):
    high = value.astype(bf16)
    return high, (value - high.astype(f32)).astype(bf16)


def partial_body(role, mine, in_inverse, out_own, other, out):
    deep = out_own.shape[0] // CORES

    @pl.when(role[0] == 0)
    def _():

        @pl.loop(0, SIDE)
        def _(i):
            high, low = high_low(dot(flat(mine[i, :, 0]), in_inverse[...], by_cols))
            out[i, 0] = high
            out[i, 1] = low

    @pl.when(role[0] == 1)
    def _():
        @pl.loop(0, SIDE)
        def _(i):
            near, far = flat(mine[i, :, 0]), flat(mine[i, :, 1])
            for half, inverse in ((0, other), (1, out_own)):
                part = dot(near, inverse[:deep], plain) + dot(far, inverse[deep:], plain)
                out[i, half] = part.astype(bf16)


def resum(first, parts):
    total = jnp.sum(parts.astype(f32), axis=0)
    whole = total[0] + total[1]
    high = lax.reduce_precision(whole, exponent_bits=8, mantissa_bits=7)
    parts = [
        jnp.where(first, high, total[0]).astype(bf16),
        jnp.where(first, whole - high, total[1]).astype(bf16),
    ]
    return jnp.stack([part.reshape(SIDE, -1, part.shape[1]) for part in parts], axis=1)


def finish_body(role, parts, out):
    totals = [sum(parts[k, half].astype(f32) for k in range(SIDE)) for half in range(CORES)]

    @pl.when(role[0] == 0)
    def _():
        out[0] = (totals[0] + totals[1]).astype(bf16)
        out[1] = jnp.zeros_like(out[1])

    @pl.when(role[0] == 1)
    def _():
        out[0] = totals[0].astype(bf16)
        out[1] = totals[1].astype(bf16)


def natural_body(tokens, role, mixed, crossed, out):
    def total(left, right):
        return sum(dot(left(i), right(i), by_rows) for i in range(SIDE)) / tokens

    @pl.when(role[0] == 0)
    def _():
        out[...] = total(lambda i: flat(mixed[i, :, 0]), lambda i: flat(crossed[i]))

    @pl.when(role[0] == 1)
    def _():
        out[...] = total(lambda i: flat(crossed[i]), lambda i: flat(mixed[i, :, 1]))


def running_body(role, mine, their, late, their_late, in_old, out_old, in_new, out_new):
    tokens = late.shape[0] * late.shape[1] * late.shape[2]
    width, wide = in_old.shape[1], out_old.shape[1]
    new_part = 1.0 - stat_decay

    def finish(in_rows, near_rows, far_rows, in_cols, out_cols):
        batch = sum(dot(in_rows(i), in_cols(i), by_rows) for i in range(SIDE)) / tokens
        in_new[...] = stat_decay * in_old[...] + new_part * batch
        for half, rows in ((0, near_rows), (1, far_rows)):
            at = pl.ds(half * wide, wide)
            batch = sum(dot(rows(i), out_cols(i), by_rows) for i in range(SIDE)) / tokens
            out_new[at, :] = stat_decay * out_old[at, :] + new_part * batch

    def part(ref, half, start=0, stop=None):
        return lambda i: flat(ref[i, :, half, :, start:stop])

    def turned(ref, spot):
        return lambda i: flat(ref[lax.rem(spot + (SIDE - i), SIDE)])

    @pl.when(role[0] == 0)
    def _():
        rows, cols = turned(their_late, role[2]), part(mine, 0, 0, width)
        finish(rows, part(their, 0), part(their, 1), cols, part(mine, 1))

    @pl.when(role[0] == 1)
    def _():
        rows, cols = turned(late, role[1]), part(their, 0, width)
        finish(rows, part(mine, 0), part(mine, 1), cols, turned(their_late, role[2]))


def per_device(
    layer_inputs, output_grads, input_factor, output_factor, input_inverse, output_inverse
):
    rows = layer_inputs.shape[0]
    wide = output_grads.shape[1]
    tokens = rows * SIDE * SIDE
    core = lax.axis_index("core")
    first = core == 0
    role = core.astype(jnp.int32).reshape(1)
    spot = (lax.axis_index("x"), lax.axis_index("y"))
    tied = lax.optimization_barrier

    out_z = role_groups("zh", "zl")
    out_xy = role_groups("x", "y")
    back_z = role_groups("zl", "zh")
    back_xy = role_groups("y", "x")

    grads_pair = lax.all_gather(output_grads, "core", axis=0, tiled=False)
    grads_moved = lax.ppermute(grads_pair, ALL, swap_pairs())
    grads_pair, layer_inputs, input_inverse = tied((grads_pair, layer_inputs, input_inverse))
    input_pair = jnp.concatenate([layer_inputs, input_inverse])
    input_pair = lax.all_gather(input_pair, "core", axis=1, tiled=True)
    input_pair, in_inverse = input_pair[:rows], input_pair[rows:]
    inputs_moved = lax.ppermute(input_pair, ALL, swap_pairs())
    block = jnp.where(first, jnp.stack([input_pair, grads_pair[0]]), grads_moved)
    block = gather(block, out_z)
    block, late, inputs_moved, other = tied(
        (block, grads_pair[1], inputs_moved, output_inverse)
    )
    mine = gather_direct(block, out_xy)
    other = core_swap(other)
    late = gather(jnp.where(first, late, inputs_moved), out_z)
    mine, late = tied((mine, late))

    part = local_call(
        partial_body,
        jax.ShapeDtypeStruct((SIDE, CORES, SIDE * rows, wide), bf16),
        role,
        mine,
        in_inverse,
        output_inverse,
        other,
        flops=2 * tokens * 4 * wide * wide,
    )
    part = exchange(part, back_xy)
    part = resum(first, part)
    part, late, mine = tied((part, late, mine))
    their = core_swap(mine)
    part = exchange(part, back_z)
    turns = [lax.ppermute(late, ALL, ring_pairs(turn)) for turn in range(1, SIDE)]
    late = jnp.stack([late] + turns)
    their_late = core_swap(late)
    part, late = tied((part, late))
    mixed = local_call(
        finish_body, jax.ShapeDtypeStruct((CORES, rows, wide), bf16), role, part
    )
    mixed = gather(mixed, back_z)
    mixed = gather_direct(mixed, back_xy)
    input_running, output_running = local_call(
        running_body,
        (
            jax.ShapeDtypeStruct(input_factor.shape, f32),
            jax.ShapeDtypeStruct(output_factor.shape, f32),
        ),
        jnp.stack([core, jnp.where(first, spot[0], spot[1]), jnp.where(first, spot[1], spot[0])]),
        mine,
        their,
        late,
        their_late,
        input_factor,
        output_factor,
        flops=2 * tokens * (2 * wide * wide + wide * wide // 2),
    )
    mixed, input_running, output_running = tied((mixed, input_running, output_running))
    crossed = core_swap(mixed[:, :, 0])
    natural_gradient = local_call(
        functools.partial(natural_body, tokens),
        jax.ShapeDtypeStruct((wide, wide), f32),
        role,
        mixed,
        crossed,
        flops=2 * tokens * wide * wide,
    )
    return (input_running, output_running, natural_gradient)


def solution(mesh):
    grid = Mesh(mesh.devices.reshape(SIDE, SIDE, SIDE, SIDE, CORES), ALL)
    spec = P(TOK, FEAT)
    return jax.shard_map(
        per_device, mesh=grid, in_specs=(spec,) * 6, out_specs=(spec,) * 3, check_vma=False
    )
```

```python
import functools
import math

import jax
import jax.numpy as jnp
from jax import lax
from jax.experimental import pallas as pl
from jax.experimental.pallas import tpu as pltpu
from jax.sharding import Mesh, PartitionSpec as P

stat_decay = 0.9
by_rows = (((0,), (0,)), ((), ()))
by_cols = (((1,), (1,)), ((), ()))
plain = (((1,), (0,)), ((), ()))
TOK = ("x", "zh")
FEAT = ("y", "zl", "core")
ALL = TOK + FEAT
SIDE = 4
CORES = 2
f32, bf16 = jnp.float32, jnp.bfloat16


def device(x, zh, y, zl, core):
    return (((x * SIDE + zh) * SIDE + y) * SIDE + zl) * CORES + core


def role_groups(first, second):
    groups = []
    for core, axis in ((0, first), (1, second)):
        others = [name for name in ALL[:4] if name != axis]
        for i in range(SIDE):
            for j in range(SIDE):
                for k in range(SIDE):
                    fixed = dict(zip(others, (i, j, k)))
                    groups.append(
                        [device(core=core, **fixed, **{axis: n}) for n in range(SIDE)]
                    )
    return groups


def swap_pairs():
    pairs = []
    for x in range(SIDE):
        for zh in range(SIDE):
            for y in range(SIDE):
                for zl in range(SIDE):
                    pairs.append((device(x, zh, y, zl, 0), device(x, zh, y, zl, 0)))
                    pairs.append((device(x, zh, y, zl, 1), device(y, zl, x, zh, 1)))
    return pairs


def ring_pairs(turn):
    pairs = []
    for group in role_groups("x", "y"):
        pairs += [(group[n], group[(n + turn) % SIDE]) for n in range(SIDE)]
    return pairs


def gather(block, groups):
    return lax.all_gather(block, ALL, axis_index_groups=groups, axis=0, tiled=False)


def exchange(parts, groups):
    return lax.all_to_all(parts, ALL, 0, 0, axis_index_groups=groups)


def gather_direct(block, groups):
    return exchange(jnp.broadcast_to(block[None], (SIDE,) + block.shape), groups)


def core_swap(block):
    return lax.ppermute(block, "core", [(0, 1), (1, 0)])


def dot(left, right, dims):
    return lax.dot_general(left, right, dims, preferred_element_type=f32)


def flat(block):
    return block.reshape(-1, block.shape[-1])


def local_call(body, out_shape, role, *operands, flops=0, steps=None, blocks=None, out_blocks=None, scratch=()):
    moved = sum(o.size * o.dtype.itemsize for o in operands)
    moved += sum(math.prod(o.shape) * o.dtype.itemsize for o in jax.tree.leaves(out_shape))
    whole = pl.BlockSpec(memory_space=pltpu.VMEM)
    if steps is None:
        grid, in_blocks = (), [whole] * len(operands)
        out_blocks = out_blocks or jax.tree.map(lambda _: whole, out_shape)
    else:
        grid, in_blocks, out_blocks = (steps,), blocks[0], blocks[1]
    return pl.pallas_call(
        body,
        grid=grid,
        out_shape=out_shape,
        in_specs=[pl.BlockSpec(memory_space=pltpu.SMEM)] + in_blocks,
        out_specs=out_blocks,
        scratch_shapes=list(scratch),
        compiler_params=pltpu.CompilerParams(vmem_limit_bytes=14 * 1024 * 1024),
        cost_estimate=pl.CostEstimate(flops=flops, bytes_accessed=moved, transcendentals=0),
    )(role, *operands)


def block_at(shape, place):
    def index(step):
        return tuple(step if axis == place else 0 for axis in range(len(shape)))

    return pl.BlockSpec(shape, index)


def high_low(value):
    high = value.astype(bf16)
    return high, (value - high.astype(f32)).astype(bf16)


def partial_body(role, mine, in_inverse, out_inverse, out):
    deep = out_inverse.shape[1] // CORES

    @pl.when(role[0] == 0)
    def _():

        @pl.loop(0, SIDE)
        def _(i):
            high, low = high_low(dot(flat(mine[i, :, 0]), in_inverse[...], by_cols))
            out[i, 0] = high
            out[i, 1] = low

    @pl.when(role[0] == 1)
    def _():
        @pl.loop(0, SIDE)
        def _(i):
            near, far = flat(mine[i, :, 0]), flat(mine[i, :, 1])
            for half in range(CORES):
                part = dot(near, out_inverse[half, :deep], plain)
                part = part + dot(far, out_inverse[half, deep:], plain)
                out[i, half] = part.astype(bf16)


def resum(first, parts):
    total = jnp.sum(parts.astype(f32), axis=0)
    whole = total[0] + total[1]
    high = lax.reduce_precision(whole, exponent_bits=8, mantissa_bits=7)
    parts = [
        jnp.where(first, high, total[0]).astype(bf16),
        jnp.where(first, whole - high, total[1]).astype(bf16),
    ]
    return jnp.stack([part.reshape(SIDE, -1, part.shape[1]) for part in parts], axis=1)


def finish_body(role, parts, out):
    totals = [sum(parts[k, half].astype(f32) for k in range(SIDE)) for half in range(CORES)]

    @pl.when(role[0] == 0)
    def _():
        out[0] = (totals[0] + totals[1]).astype(bf16)
        out[1] = jnp.zeros_like(out[1])

    @pl.when(role[0] == 1)
    def _():
        out[0] = totals[0].astype(bf16)
        out[1] = totals[1].astype(bf16)


def natural_body(tokens, role, mixed, crossed, out):
    def total(left, right):
        return sum(dot(left(i), right(i), by_rows) for i in range(SIDE)) / tokens

    @pl.when(role[0] == 0)
    def _():
        out[...] = total(lambda i: flat(mixed[i, :, 0]), lambda i: flat(crossed[i]))

    @pl.when(role[0] == 1)
    def _():
        out[...] = total(lambda i: flat(crossed[i]), lambda i: flat(mixed[i, :, 1]))


def running_body(role, mine, their, late, their_late, in_old, out_old, in_new, out_new):
    tokens = late.shape[0] * late.shape[1] * late.shape[2]
    width, wide = in_old.shape[1], out_old.shape[1]
    new_part = 1.0 - stat_decay

    def finish(in_rows, near_rows, far_rows, in_cols, out_cols):
        batch = sum(dot(in_rows(i), in_cols(i), by_rows) for i in range(SIDE)) / tokens
        in_new[...] = stat_decay * in_old[...] + new_part * batch
        for half, rows in ((0, near_rows), (1, far_rows)):
            at = pl.ds(half * wide, wide)
            batch = sum(dot(rows(i), out_cols(i), by_rows) for i in range(SIDE)) / tokens
            out_new[at, :] = stat_decay * out_old[at, :] + new_part * batch

    def part(ref, half, start=0, stop=None):
        return lambda i: flat(ref[i, :, half, :, start:stop])

    def turned(ref, spot):
        return lambda i: flat(ref[lax.rem(spot + (SIDE - i), SIDE)])

    @pl.when(role[0] == 0)
    def _():
        rows, cols = turned(their_late, role[2]), part(mine, 0, 0, width)
        finish(rows, part(their, 0), part(their, 1), cols, part(mine, 1))

    @pl.when(role[0] == 1)
    def _():
        rows, cols = turned(late, role[1]), part(their, 0, width)
        finish(rows, part(mine, 0), part(mine, 1), cols, turned(their_late, role[2]))


def per_device(
    layer_inputs, output_grads, input_factor, output_factor, input_inverse, output_inverse
):
    rows = layer_inputs.shape[0]
    wide = output_grads.shape[1]
    tokens = rows * SIDE * SIDE
    core = lax.axis_index("core")
    first = core == 0
    role = core.astype(jnp.int32).reshape(1)
    spot = (lax.axis_index("x"), lax.axis_index("y"))
    tied = lax.optimization_barrier

    out_z = role_groups("zh", "zl")
    out_xy = role_groups("x", "y")
    back_z = role_groups("zl", "zh")
    back_xy = role_groups("y", "x")

    grads_pair = lax.all_gather(output_grads, "core", axis=0, tiled=False)
    input_pair = jnp.concatenate([layer_inputs, input_inverse])
    input_pair = lax.all_gather(input_pair, "core", axis=1, tiled=True)
    grads_pair, input_pair = tied((grads_pair, input_pair))
    input_pair, in_inverse = input_pair[:rows], input_pair[rows:]
    moved = jnp.concatenate([grads_pair, input_pair[None]])
    output_inverse, moved = tied((output_inverse, moved))
    moved = lax.ppermute(moved, ALL, swap_pairs())
    out_inverse = lax.all_gather(output_inverse, "core", axis=0, tiled=False)
    moved, grads_pair, out_inverse = tied((moved, grads_pair, out_inverse))
    grads_moved, inputs_moved = moved[:CORES], moved[CORES]
    block = jnp.where(first, jnp.stack([input_pair, grads_pair[0]]), grads_moved)
    block = gather(block, out_z)
    block, late, inputs_moved = tied((block, grads_pair[1], inputs_moved))
    mine = gather_direct(block, out_xy)
    late = gather(jnp.where(first, late, inputs_moved), out_z)
    mine, late = tied((mine, late))

    part = local_call(
        partial_body,
        jax.ShapeDtypeStruct((SIDE, CORES, SIDE * rows, wide), bf16),
        role,
        mine,
        in_inverse,
        out_inverse,
        flops=2 * tokens * 4 * wide * wide,
    )
    part = exchange(part, back_xy)
    part = resum(first, part)
    part, late, mine = tied((part, late, mine))
    their = core_swap(mine)
    part = exchange(part, back_z)
    turns = [lax.ppermute(late, ALL, ring_pairs(turn)) for turn in range(1, SIDE)]
    late = jnp.stack([late] + turns)
    their_late = core_swap(late)
    part, late = tied((part, late))
    mixed = local_call(
        finish_body, jax.ShapeDtypeStruct((CORES, rows, wide), bf16), role, part
    )
    mixed = gather(mixed, back_z)
    mixed = gather_direct(mixed, back_xy)
    input_running, output_running = local_call(
        running_body,
        (
            jax.ShapeDtypeStruct(input_factor.shape, f32),
            jax.ShapeDtypeStruct(output_factor.shape, f32),
        ),
        jnp.stack([core, jnp.where(first, spot[0], spot[1]), jnp.where(first, spot[1], spot[0])]),
        mine,
        their,
        late,
        their_late,
        input_factor,
        output_factor,
        flops=2 * tokens * (2 * wide * wide + wide * wide // 2),
    )
    mixed, input_running, output_running = tied((mixed, input_running, output_running))
    crossed = core_swap(mixed[:, :, 0])
    natural_gradient = local_call(
        functools.partial(natural_body, tokens),
        jax.ShapeDtypeStruct((wide, wide), f32),
        role,
        mixed,
        crossed,
        flops=2 * tokens * wide * wide,
    )
    return (input_running, output_running, natural_gradient)


def solution(mesh):
    grid = Mesh(mesh.devices.reshape(SIDE, SIDE, SIDE, SIDE, CORES), ALL)
    spec = P(TOK, FEAT)
    return jax.shard_map(
        per_device, mesh=grid, in_specs=(spec,) * 6, out_specs=(spec,) * 3, check_vma=False
    )
```

```python
import functools
import math

import jax
import jax.numpy as jnp
from jax import lax
from jax.experimental import pallas as pl
from jax.experimental.pallas import tpu as pltpu
from jax.sharding import Mesh, PartitionSpec as P

stat_decay = 0.9
by_rows = (((0,), (0,)), ((), ()))
by_cols = (((1,), (1,)), ((), ()))
plain = (((1,), (0,)), ((), ()))
TOK = ("x", "zh")
FEAT = ("y", "zl", "core")
ALL = TOK + FEAT
SIDE = 4
CORES = 2
f32, bf16 = jnp.float32, jnp.bfloat16


def device(x, zh, y, zl, core):
    return (((x * SIDE + zh) * SIDE + y) * SIDE + zl) * CORES + core


def role_groups(first, second):
    groups = []
    for core, axis in ((0, first), (1, second)):
        others = [name for name in ALL[:4] if name != axis]
        for i in range(SIDE):
            for j in range(SIDE):
                for k in range(SIDE):
                    fixed = dict(zip(others, (i, j, k)))
                    groups.append(
                        [device(core=core, **fixed, **{axis: n}) for n in range(SIDE)]
                    )
    return groups


def swap_pairs():
    pairs = []
    for x in range(SIDE):
        for zh in range(SIDE):
            for y in range(SIDE):
                for zl in range(SIDE):
                    pairs.append((device(x, zh, y, zl, 0), device(x, zh, y, zl, 0)))
                    pairs.append((device(x, zh, y, zl, 1), device(y, zl, x, zh, 1)))
    return pairs


def ring_pairs(turn):
    pairs = []
    for group in role_groups("x", "y"):
        pairs += [(group[n], group[(n + turn) % SIDE]) for n in range(SIDE)]
    return pairs


def gather(block, groups):
    return lax.all_gather(block, ALL, axis_index_groups=groups, axis=0, tiled=False)


def exchange(parts, groups):
    return lax.all_to_all(parts, ALL, 0, 0, axis_index_groups=groups)


def gather_direct(block, groups):
    return exchange(jnp.broadcast_to(block[None], (SIDE,) + block.shape), groups)


def core_swap(block):
    return lax.ppermute(block, "core", [(0, 1), (1, 0)])


def dot(left, right, dims):
    return lax.dot_general(left, right, dims, preferred_element_type=f32)


def flat(block):
    return block.reshape(-1, block.shape[-1])


def local_call(body, out_shape, role, *operands, flops=0, steps=None, blocks=None, out_blocks=None, scratch=()):
    moved = sum(o.size * o.dtype.itemsize for o in operands)
    moved += sum(math.prod(o.shape) * o.dtype.itemsize for o in jax.tree.leaves(out_shape))
    whole = pl.BlockSpec(memory_space=pltpu.VMEM)
    if steps is None:
        grid, in_blocks = (), [whole] * len(operands)
        out_blocks = out_blocks or jax.tree.map(lambda _: whole, out_shape)
    else:
        grid, in_blocks, out_blocks = (steps,), blocks[0], blocks[1]
    return pl.pallas_call(
        body,
        grid=grid,
        out_shape=out_shape,
        in_specs=[pl.BlockSpec(memory_space=pltpu.SMEM)] + in_blocks,
        out_specs=out_blocks,
        scratch_shapes=list(scratch),
        compiler_params=pltpu.CompilerParams(vmem_limit_bytes=14 * 1024 * 1024),
        cost_estimate=pl.CostEstimate(flops=flops, bytes_accessed=moved, transcendentals=0),
    )(role, *operands)


def block_at(shape, place):
    def index(step):
        return tuple(step if axis == place else 0 for axis in range(len(shape)))

    return pl.BlockSpec(shape, index)


def high_low(value):
    high = value.astype(bf16)
    return high, (value - high.astype(f32)).astype(bf16)


def partial_body(role, mine, in_inverse, out_inverse, out):
    deep = out_inverse.shape[1] // CORES

    @pl.when(role[0] == 0)
    def _():

        @pl.loop(0, SIDE)
        def _(i):
            high, low = high_low(dot(flat(mine[i, :, 0]), in_inverse[...], by_cols))
            out[i, 0] = high
            out[i, 1] = low

    @pl.when(role[0] == 1)
    def _():
        @pl.loop(0, SIDE)
        def _(i):
            near, far = flat(mine[i, :, 0]), flat(mine[i, :, 1])
            for half in range(CORES):
                part = dot(near, out_inverse[half, :deep], plain)
                part = part + dot(far, out_inverse[half, deep:], plain)
                out[i, half] = part.astype(bf16)


def resum(first, parts):
    total = jnp.sum(parts.astype(f32), axis=0)
    whole = total[0] + total[1]
    high = lax.reduce_precision(whole, exponent_bits=8, mantissa_bits=7)
    parts = [
        jnp.where(first, high, total[0]).astype(bf16),
        jnp.where(first, whole - high, total[1]).astype(bf16),
    ]
    return jnp.stack([part.reshape(SIDE, -1, part.shape[1]) for part in parts], axis=1)


def finish(first, parts):
    total = jnp.sum(parts.astype(f32), axis=0)
    near = jnp.where(first, total[0] + total[1], total[0])
    far = jnp.where(first, jnp.zeros_like(total[1]), total[1])
    return jnp.stack([near, far]).astype(bf16)


def natural_body(tokens, role, mixed, crossed, out):
    def total(left, right):
        return sum(dot(left(i), right(i), by_rows) for i in range(SIDE)) / tokens

    @pl.when(role[0] == 0)
    def _():
        out[...] = total(lambda i: flat(mixed[i, :, 0]), lambda i: flat(crossed[i]))

    @pl.when(role[0] == 1)
    def _():
        out[...] = total(lambda i: flat(crossed[i]), lambda i: flat(mixed[i, :, 1]))


def running_body(role, mine, their, late, their_late, in_old, out_old, in_new, out_new):
    tokens = late.shape[0] * late.shape[1] * late.shape[2]
    width, wide = in_old.shape[1], out_old.shape[1]
    new_part = 1.0 - stat_decay

    def finish(in_rows, near_rows, far_rows, in_cols, out_cols):
        batch = sum(dot(in_rows(i), in_cols(i), by_rows) for i in range(SIDE)) / tokens
        in_new[...] = stat_decay * in_old[...] + new_part * batch
        for half, rows in ((0, near_rows), (1, far_rows)):
            at = pl.ds(half * wide, wide)
            batch = sum(dot(rows(i), out_cols(i), by_rows) for i in range(SIDE)) / tokens
            out_new[at, :] = stat_decay * out_old[at, :] + new_part * batch

    def part(ref, half, start=0, stop=None):
        return lambda i: flat(ref[i, :, half, :, start:stop])

    def turned(ref, spot):
        return lambda i: flat(ref[lax.rem(spot + (SIDE - i), SIDE)])

    @pl.when(role[0] == 0)
    def _():
        rows, cols = turned(their_late, role[2]), part(mine, 0, 0, width)
        finish(rows, part(their, 0), part(their, 1), cols, part(mine, 1))

    @pl.when(role[0] == 1)
    def _():
        rows, cols = turned(late, role[1]), part(their, 0, width)
        finish(rows, part(mine, 0), part(mine, 1), cols, turned(their_late, role[2]))


def per_device(
    layer_inputs, output_grads, input_factor, output_factor, input_inverse, output_inverse
):
    rows = layer_inputs.shape[0]
    wide = output_grads.shape[1]
    tokens = rows * SIDE * SIDE
    core = lax.axis_index("core")
    first = core == 0
    role = core.astype(jnp.int32).reshape(1)
    spot = (lax.axis_index("x"), lax.axis_index("y"))
    tied = lax.optimization_barrier

    out_z = role_groups("zh", "zl")
    out_xy = role_groups("x", "y")
    back_z = role_groups("zl", "zh")
    back_xy = role_groups("y", "x")

    grads_pair = lax.all_gather(output_grads, "core", axis=0, tiled=False)
    input_pair = jnp.concatenate([layer_inputs, input_inverse])
    input_pair = lax.all_gather(input_pair, "core", axis=1, tiled=True)
    grads_pair, input_pair = tied((grads_pair, input_pair))
    input_pair, in_inverse = input_pair[:rows], input_pair[rows:]
    moved = jnp.concatenate([grads_pair, input_pair[None]])
    output_inverse, moved = tied((output_inverse, moved))
    moved = lax.ppermute(moved, ALL, swap_pairs())
    out_inverse = lax.all_gather(output_inverse, "core", axis=0, tiled=False)
    moved, grads_pair, out_inverse = tied((moved, grads_pair, out_inverse))
    grads_moved, inputs_moved = moved[:CORES], moved[CORES]
    block = jnp.where(first, jnp.stack([input_pair, grads_pair[0]]), grads_moved)
    block = gather(block, out_z)
    block, late, inputs_moved = tied((block, grads_pair[1], inputs_moved))
    mine = gather_direct(block, out_xy)
    late = gather(jnp.where(first, late, inputs_moved), out_z)
    mine, late = tied((mine, late))

    part = local_call(
        partial_body,
        jax.ShapeDtypeStruct((SIDE, CORES, SIDE * rows, wide), bf16),
        role,
        mine,
        in_inverse,
        out_inverse,
        flops=2 * tokens * 4 * wide * wide,
    )
    part = exchange(part, back_xy)
    part = resum(first, part)
    part, late, mine = tied((part, late, mine))
    their = core_swap(mine)
    part = exchange(part, back_z)
    turns = [lax.ppermute(late, ALL, ring_pairs(turn)) for turn in range(1, SIDE)]
    late = jnp.stack([late] + turns)
    their_late = core_swap(late)
    part, late = tied((part, late))
    mixed = finish(first, part)
    mixed = gather(mixed, back_z)
    mixed = gather_direct(mixed, back_xy)
    input_running, output_running = local_call(
        running_body,
        (
            jax.ShapeDtypeStruct(input_factor.shape, f32),
            jax.ShapeDtypeStruct(output_factor.shape, f32),
        ),
        jnp.stack([core, jnp.where(first, spot[0], spot[1]), jnp.where(first, spot[1], spot[0])]),
        mine,
        their,
        late,
        their_late,
        input_factor,
        output_factor,
        flops=2 * tokens * (2 * wide * wide + wide * wide // 2),
    )
    mixed, input_running, output_running = tied((mixed, input_running, output_running))
    crossed = core_swap(mixed[:, :, 0])
    natural_gradient = local_call(
        functools.partial(natural_body, tokens),
        jax.ShapeDtypeStruct((wide, wide), f32),
        role,
        mixed,
        crossed,
        flops=2 * tokens * wide * wide,
    )
    return (input_running, output_running, natural_gradient)


def solution(mesh):
    grid = Mesh(mesh.devices.reshape(SIDE, SIDE, SIDE, SIDE, CORES), ALL)
    spec = P(TOK, FEAT)
    return jax.shard_map(
        per_device, mesh=grid, in_specs=(spec,) * 6, out_specs=(spec,) * 3, check_vma=False
    )
```
